512 devices in a mesh: row: 32 (over z, core), col: 16 (over x, y).
Axes of the slice: x: 4, y: 4, z: 16, core: 2. Of those that a mesh axis runs over, the one named last changes fastest.
Arguments:
- slab: float32 [32768, 8192], P('row', 'col'), may hold values from -6 to 6
- reflectors: float32 [32768, 64], P('row', 'col'), as said below
- sketch: float32 [128, 32768], P(None, 'row'), may hold values from -0.5 to 0.5
Outputs:
- updated: float32 [32768, 8192], P('row', 'col')
- coupled: float32 [64, 8192], P(None, 'col')
- sketch_next: float32 [128, 8192], P(None, 'col')
The draws below stay inside these ranges and needn't reach their ends.
Inputs may be any that keep to these rules, and one draw needn't show every extreme that they name: `reflectors`: each column's squared length is near 2, and columns are correlated.
All inputs are finite; a program needn't handle non-finite values.
Results may differ from the reference program's by a relative error of at most 0.00017.
Values sent between devices are 32-bit elements; how exact they have to be, the bound alone decides.
No kernel may reach another device: no remote copies, remote signals or barrier semaphores. Data moves between devices by JAX's collectives and lax.ppermute only.
A program may use at most 64 MiB of HBM per device.

```python
import jax
import jax.numpy as jnp
from jax import lax

PANEL = 64
SKETCH = 128
TOTAL_ROWS = 32768
NC = 8192


def draw_reflectors(key, part):
    key = jax.random.fold_in(key, 7)
    first, second = jax.random.split(key)
    own = jax.random.normal(first, (TOTAL_ROWS, PANEL), jnp.float32)
    common = jax.random.normal(second, (TOTAL_ROWS, 1), jnp.float32)
    mixed = own + 0.5 * common
    scale = (2.0 / (1.25 * TOTAL_ROWS)) ** 0.5
    return (mixed * scale).astype(jnp.float32)


def block_scale(rng, dims, cuts, least, largest):
    level = 1.0
    for position, blocks in cuts:
        steps = jax.random.uniform(jax.random.fold_in(jax.random.fold_in(rng, 6), position), (blocks,), jnp.float32, least / len(cuts), largest / len(cuts))
        level = level * jnp.repeat(jnp.exp(steps), dims[position] // blocks).reshape((-1,) + (1,) * (len(dims) - 1 - position))
    return level


def scatter_about(key, shape, width, bound, shards=(), dtype=jnp.bfloat16):
    entries = width * jax.random.normal(key, shape, jnp.float32)
    if shards:
        entries = entries * block_scale(key, shape, shards, -0.22, 0.18)
    return jnp.clip(entries, -bound, bound).astype(dtype)


def setup_inputs(seed: int = 0) -> dict:
    splits = jax.random.split(jax.random.key(seed), 4)
    return {
        "slab": scatter_about(splits[0], (TOTAL_ROWS, NC), 1.0, 6.0, ((0, 32), (1, 16)), jnp.float32),
        "reflectors": draw_reflectors(jax.random.fold_in(splits[3], 71), 0),
        "sketch": scatter_about(splits[2], (SKETCH, TOTAL_ROWS), SKETCH ** -0.5, 0.5, ((1, 32),), jnp.float32),
    }


def matmul(left, right):
    return jnp.dot(left.astype(jnp.float32), right.astype(jnp.float32), precision=lax.Precision.HIGHEST, preferred_element_type=jnp.float32)

def reference(slab, reflectors, sketch):
    panel_sketch = matmul(sketch, reflectors)
    gram = matmul(panel_sketch.T, panel_sketch)
    lower_inverse = jnp.tril(gram, -1) + jnp.diag(0.5 * jnp.diagonal(gram))
    projection = matmul(reflectors.T, slab)
    coupled = lax.linalg.triangular_solve(lower_inverse, projection, left_side=True, lower=True)
    updated = slab - matmul(reflectors, coupled)
    sketch_next = matmul(sketch, updated) * (SKETCH / TOTAL_ROWS) ** 0.5
    return (updated, coupled, sketch_next)
```

```python
import jax
import jax.numpy as jnp
from jax import lax
from jax.experimental import pallas as pl
from jax.experimental.pallas import tpu as pltpu
from jax.sharding import Mesh, PartitionSpec as P

CORES = 2
NEAR = 2
CHUNKS = 4
LANES = 128
PAIR = 2
LARGE_VMEM = 58 * 1024 * 1024
SMALL_VMEM = 8 * 1024 * 1024
HIGHEST = lax.Precision.HIGHEST
SWAP = [(0, 1), (1, 0)]


def contract(left, right, left_dim, right_dim):
    return lax.dot_general(left, right, (((left_dim,), (right_dim,)), ((), ())), precision=HIGHEST, preferred_element_type=jnp.float32)


def start_loads(source, target, sems):
    step = source.shape[0] // CHUNKS
    copies = []
    for k in range(CHUNKS):
        rows = pl.ds(k * step, step)
        copies.append(pltpu.make_async_copy(source.at[rows, :], target.at[rows, :], sems.at[k]))
        copies[-1].start()
    return copies


def lay_panel(gathered_ref, panel_ref):
    own = gathered_ref.shape[1]
    for k in range(gathered_ref.shape[0]):
        panel_ref[k * own:(k + 1) * own, :] = gathered_ref[k]


def times_slab(left, slab_ref, copies):
    step = slab_ref.shape[0] // CHUNKS
    total = None
    for k in range(CHUNKS):
        copies[k].wait()
        term = contract(left[:, k * step:(k + 1) * step], slab_ref[k * step:(k + 1) * step, :], 1, 0)
        total = term if total is None else total + term
    return total


def sketch_slab_kernel(sketch_ref, slab_hbm, out_ref, slab_ref, sems):
    copies = start_loads(slab_hbm, slab_ref, sems)
    out_ref[...] = times_slab(sketch_ref[...], slab_ref, copies)


def products_kernel(place_ref, gathered_ref, sketch_ref, sketch_slab_ref, slab_hbm, mine_ref, other_ref, slab_ref, panel_ref, blocks_ref, sems):
    copies = start_loads(slab_hbm, slab_ref, sems)
    lay_panel(gathered_ref, panel_ref)
    panel = panel_ref.shape[0]
    sketch_rows = sketch_ref.shape[0]
    blocks = blocks_ref.shape[0]
    folded = panel // blocks
    top = sketch_rows + panel
    panel_sketch = contract(panel_ref[...], sketch_ref[...], 1, 1)
    projection = times_slab(panel_ref[...], slab_ref, copies)
    for j in range(blocks):
        columns = slice(j * LANES, (j + 1) * LANES)
        blocks_ref[j, :sketch_rows, :] = sketch_slab_ref[:, columns]
        blocks_ref[j, sketch_rows:top, :] = projection[:, columns]
        blocks_ref[j, top:, :] = panel_sketch[j * folded:(j + 1) * folded, :]
    half = mine_ref.shape[0]
    core = place_ref[0]
    for out, first in ((other_ref, (1 - core) * half), (mine_ref, core * half)):
        for t in range(half):
            for i in range(out.shape[1]):
                out[t, i] = blocks_ref[first + t, PAIR * i:PAIR * (i + 1), :]


def split_kernel(place_ref, mine_ref, got_ref, keep_ref, send_ref):
    near = place_ref[1]
    send_ref[...] = mine_ref[1 - near] + got_ref[1 - near]
    keep_ref[...] = mine_ref[near] + got_ref[near]


def add_kernel(left_ref, right_ref, out_ref):
    out_ref[...] = left_ref[...] + right_ref[...]


def sum_kernel(parts_ref, out_ref):
    total = parts_ref[0]
    for k in range(1, parts_ref.shape[0]):
        total = total + parts_ref[k]
    for k in range(out_ref.shape[0]):
        out_ref[k] = total


def stack_kernel(first_ref, second_ref, out_ref):
    out_ref[0] = first_ref[...]
    out_ref[1] = second_ref[...]


def update_kernel(scale, place_ref, mine_ref, other_ref, gathered_ref, slab_hbm, updated_hbm, coupled_ref, sketch_next_ref,
                  slab_ref, updated_ref, panel_ref, blocks_ref, in_sems, out_sems):
    loads = start_loads(slab_hbm, slab_ref, in_sems)
    core, near = place_ref[0], place_ref[1]
    sketch_rows, columns = sketch_next_ref.shape
    panel, depth = panel_ref.shape
    step = depth // CHUNKS
    for ref, owner in ((mine_ref, core), (other_ref, 1 - core)):
        for t, side in ((0, near), (1, 1 - near)):
            block = owner * NEAR + side
            for i in range(ref.shape[1]):
                blocks_ref[block, PAIR * i:PAIR * (i + 1), :] = ref[t, i]
    lay_panel(gathered_ref, panel_ref)
    blocks = blocks_ref.shape[0]
    top = sketch_rows + panel
    panel_sketch = jnp.concatenate([blocks_ref[j, top:, :] for j in range(blocks)], axis=0)
    gram = contract(panel_sketch, panel_sketch, 1, 1)
    row = lax.broadcasted_iota(jnp.int32, gram.shape, 0)
    column = lax.broadcasted_iota(jnp.int32, gram.shape, 1)
    strict = jnp.where(row > column, gram, 0.0)
    diagonal = jnp.sum(jnp.where(row == column, gram, 0.0), axis=1, keepdims=True) * 0.5
    inverse = 1.0 / diagonal
    tiles = panel // 8
    values = [jnp.concatenate([blocks_ref[j, sketch_rows + 8 * b:sketch_rows + 8 * b + 8, :] for j in range(blocks)], axis=1)
              for b in range(tiles)]
    scales = [jnp.broadcast_to(inverse[8 * b:8 * b + 8, :], (8, columns)) for b in range(tiles)]
    for i in range(panel):
        b, r = divmod(i, 8)
        solved = values[b][r:r + 1, :] * scales[b][r:r + 1, :]
        for later in range(b, tiles):
            values[later] = values[later] - strict[8 * later:8 * later + 8, i:i + 1] * solved
    coupled = jnp.concatenate([values[b] * scales[b] for b in range(tiles)], axis=0)
    coupled_ref[...] = coupled
    stores = []
    for k in range(CHUNKS):
        rows = pl.ds(k * step, step)
        loads[k].wait()
        moved = contract(panel_ref[:, k * step:(k + 1) * step], coupled, 0, 0)
        updated_ref[k * step:(k + 1) * step, :] = slab_ref[k * step:(k + 1) * step, :] - moved
        stores.append(pltpu.make_async_copy(updated_ref.at[rows, :], updated_hbm.at[rows, :], out_sems.at[k]))
        stores[-1].start()
    correction = contract(panel_sketch, coupled, 0, 0)
    for j in range(blocks):
        lanes = slice(j * LANES, (j + 1) * LANES)
        sketch_next_ref[:, lanes] = (blocks_ref[j, :sketch_rows, :] - correction[:, lanes]) * scale
    for copy in stores:
        copy.wait()


def local(slab, reflectors, sketch):
    depth, columns = slab.shape
    sketch_rows = sketch.shape[0]
    cols, far = lax.axis_size("col"), lax.axis_size("far")
    own = reflectors.shape[1]
    panel = own * cols
    total_rows = depth * far * NEAR * CORES
    blocks = columns // LANES
    place = jnp.stack([lax.axis_index("core"), lax.axis_index("near")]).astype(jnp.int32)
    vmem, smem, hbm = (pl.BlockSpec(memory_space=space) for space in (pltpu.VMEM, pltpu.SMEM, pl.ANY))
    f32 = jnp.float32

    def call(kernel, name, out, in_specs, out_specs=vmem, scratch=(), flops=0, moved=0, grant=LARGE_VMEM):
        shapes = jax.tree.map(lambda shape: jax.ShapeDtypeStruct(shape, f32), out, is_leaf=lambda leaf: isinstance(leaf, tuple))
        return pl.pallas_call(
            kernel, out_shape=shapes, in_specs=in_specs, out_specs=out_specs, scratch_shapes=list(scratch),
            compiler_params=pltpu.CompilerParams(vmem_limit_bytes=grant),
            cost_estimate=pl.CostEstimate(flops=flops, bytes_accessed=moved, transcendentals=0), name=name)

    dma = pltpu.SemaphoreType.DMA((CHUNKS,))
    whole = pltpu.VMEM((depth, columns), f32)
    slab_bytes = depth * columns * 4

    spread = jnp.broadcast_to(reflectors.T[None], (cols, own, depth))
    gathered = lax.all_to_all(spread, "col", 0, 0, tiled=True)
    sketch_slab = call(
        sketch_slab_kernel, "sketch_slab", (sketch_rows, columns), [vmem, hbm], scratch=[whole, dma],
        flops=12 * sketch_rows * depth * columns, moved=slab_bytes)(sketch, slab)

    rows = sketch_rows + panel + panel // blocks
    pairs = rows // PAIR
    half = blocks // CORES
    mine, other = call(
        products_kernel, "products", [(half, pairs, PAIR, LANES)] * 2, [smem, vmem, vmem, vmem, hbm], [vmem, vmem],
        [whole, pltpu.VMEM((panel, depth), f32), pltpu.VMEM((blocks, rows, LANES), f32), dma],
        flops=12 * panel * depth * columns, moved=slab_bytes)(place, gathered, sketch, sketch_slab, slab)

    quarter = (pairs, PAIR, LANES)
    got = lax.ppermute(other, "core", SWAP)
    keep, send = call(split_kernel, "add_cores", [quarter] * 2, [smem, vmem, vmem], [vmem, vmem], grant=SMALL_VMEM)(place, mine, got)
    got = lax.ppermute(send, "near", SWAP)
    parts = call(add_kernel, "add_chips", quarter, [vmem, vmem], grant=SMALL_VMEM)(keep, got).reshape(far, pairs // far, PAIR, LANES)
    parts = lax.all_to_all(parts, "far", 0, 0, tiled=True)
    summed = call(sum_kernel, "sum_parts", parts.shape, [vmem], grant=SMALL_VMEM)(parts)
    first = lax.all_to_all(summed, "far", 0, 0, tiled=True).reshape(quarter)
    second = lax.ppermute(first, "near", SWAP)
    mine = call(stack_kernel, "stack", (2, *quarter), [vmem, vmem], grant=SMALL_VMEM)(first, second)
    other = lax.ppermute(mine, "core", SWAP)

    scale = (sketch_rows / total_rows) ** 0.5
    updated, coupled, sketch_next = call(
        lambda *refs: update_kernel(scale, *refs), "solve_update", [slab.shape, (panel, columns), (sketch_rows, columns)],
        [smem, vmem, vmem, vmem, hbm], [hbm, vmem, vmem],
        [whole, whole, pltpu.VMEM((panel, depth), f32), pltpu.VMEM((blocks, rows, LANES), f32), dma, dma],
        flops=12 * panel * depth * columns, moved=2 * slab_bytes)(place, mine, other, gathered, slab)
    return (updated, coupled, sketch_next)


def solution(mesh):
    split = Mesh(mesh.devices.reshape(-1, NEAR, CORES, mesh.devices.shape[1]), ("far", "near", "core", "col"))
    row = ("far", "near", "core")
    in_specs = (P(row, "col"), P(row, "col"), P(None, row))
    out_specs = (P(row, "col"), P(None, "col"), P(None, "col"))
    return jax.shard_map(local, mesh=split, in_specs=in_specs, out_specs=out_specs, check_vma=False)
```

```python
import jax
import jax.numpy as jnp
from jax import lax
from jax.experimental import pallas as pl
from jax.experimental.pallas import tpu as pltpu
from jax.sharding import Mesh, PartitionSpec as P

CORES = 2
CHUNKS = 4
LANES = 128
PAIR = 2
LARGE_VMEM = 52 * 1024 * 1024
SMALL_VMEM = 8 * 1024 * 1024
HIGHEST = lax.Precision.HIGHEST
SWAP = [(0, 1), (1, 0)]


def contract(left, right, left_dim, right_dim, precision=None):
    return lax.dot_general(left, right, (((left_dim,), (right_dim,)), ((), ())), precision=precision, preferred_element_type=jnp.float32)


def parts_of(value):
    high = value.astype(jnp.bfloat16)
    return high, (value - high.astype(jnp.float32)).astype(jnp.bfloat16)


def start_loads(source, target, sems):
    step = source.shape[0] // CHUNKS
    copies = []
    for k in range(CHUNKS):
        rows = pl.ds(k * step, step)
        copies.append(pltpu.make_async_copy(source.at[rows, :], target.at[rows, :], sems.at[k]))
        copies[-1].start()
    return copies


def lay_panel(gathered_ref, panel_ref):
    own = gathered_ref.shape[1]
    for k in range(gathered_ref.shape[0]):
        panel_ref[k * own:(k + 1) * own, :] = gathered_ref[k, :, :panel_ref.shape[1]]


def spread_kernel(own_ref, out_ref):
    for k in range(out_ref.shape[0]):
        out_ref[k] = own_ref[...]


def sketch_slab_kernel(sketch_ref, slab_hbm, out_ref, high_ref, low_ref, slab_ref, sems):
    copies = start_loads(slab_hbm, slab_ref, sems)
    step = slab_ref.shape[0] // CHUNKS
    total = None
    for k in range(CHUNKS):
        copies[k].wait()
        rows = slice(k * step, (k + 1) * step)
        high, low = parts_of(slab_ref[rows, :])
        high_ref[rows, :] = high
        low_ref[rows, :] = low
        term = contract(sketch_ref[:, rows], slab_ref[rows, :], 1, 0, HIGHEST)
        total = term if total is None else total + term
    out_ref[...] = total


def products_kernel(core_ref, gathered_ref, sketch_ref, sketch_slab_ref, high_ref, low_ref, mine_ref, other_ref, panel_ref, blocks_ref):
    lay_panel(gathered_ref, panel_ref)
    panel = panel_ref.shape[0]
    sketch_rows = sketch_ref.shape[0]
    blocks = blocks_ref.shape[0]
    folded = panel // blocks
    top = sketch_rows + panel
    panel_high, panel_low = parts_of(panel_ref[...])
    both = jnp.concatenate([panel_high, panel_low], axis=0)
    sketch_high, sketch_low = parts_of(sketch_ref[...])
    wide = contract(both, sketch_high, 1, 1)
    panel_sketch = wide[:panel] + (wide[panel:] + contract(panel_high, sketch_low, 1, 1))
    wide = contract(both, high_ref[...], 1, 0)
    projection = wide[:panel] + (wide[panel:] + contract(panel_high, low_ref[...], 1, 0))
    for j in range(blocks):
        columns = slice(j * LANES, (j + 1) * LANES)
        blocks_ref[j, :sketch_rows, :] = sketch_slab_ref[:, columns]
        blocks_ref[j, sketch_rows:top, :] = projection[:, columns]
        blocks_ref[j, top:, :] = panel_sketch[j * folded:(j + 1) * folded, :]
    half = blocks // CORES
    pairs = blocks_ref.shape[1] // PAIR
    core = core_ref[0]
    for out, first in ((other_ref, (1 - core) * half), (mine_ref, core * half)):
        for t in range(half):
            for i in range(pairs):
                out[t * pairs + i] = blocks_ref[first + t, PAIR * i:PAIR * (i + 1), :]


def add_kernel(left_ref, right_ref, out_ref):
    out_ref[...] = left_ref[...] + right_ref[...]


def stack_kernel(first, after_ref, gathered_ref, out_ref, panel_ref):
    del after_ref
    own = gathered_ref.shape[1]
    count = out_ref.shape[0]
    for k in range(gathered_ref.shape[0]):
        panel_ref[k * own:(k + 1) * own, :] = gathered_ref[k, :, first:first + count]
    value = panel_ref[...]
    high = value.astype(jnp.bfloat16).astype(jnp.float32)
    out_ref[...] = jnp.concatenate([high, value - high, high], axis=0).T.astype(jnp.bfloat16)


def sum_kernel(parts_ref, after_ref, out_ref):
    del after_ref
    total = parts_ref[0]
    for k in range(1, parts_ref.shape[0]):
        total = total + parts_ref[k]
    for k in range(out_ref.shape[0]):
        out_ref[k] = total


def pass_kernel(value_ref, after_ref, out_ref):
    del after_ref
    out_ref[...] = value_ref[...]


def update_kernel(scale, core_ref, mine_ref, other_ref, top_stack_ref, low_stack_ref, slab_hbm, updated_hbm, coupled_ref, sketch_next_ref,
                  slab_ref, updated_ref, blocks_ref, in_sems, out_sems):
    loads = start_loads(slab_hbm, slab_ref, in_sems)
    core = core_ref[0]
    sketch_rows, columns = sketch_next_ref.shape
    panel = coupled_ref.shape[0]
    blocks = blocks_ref.shape[0]
    half = blocks // CORES
    pairs = blocks_ref.shape[1] // PAIR
    for ref, owner in ((mine_ref, core), (other_ref, 1 - core)):
        for t in range(half):
            for i in range(pairs):
                blocks_ref[owner * half + t, PAIR * i:PAIR * (i + 1), :] = ref[t * pairs + i]
    top = sketch_rows + panel
    panel_sketch = jnp.concatenate([blocks_ref[j, top:, :] for j in range(blocks)], axis=0)
    gram = contract(panel_sketch, panel_sketch, 1, 1, HIGHEST)
    row = lax.broadcasted_iota(jnp.int32, gram.shape, 0)
    column = lax.broadcasted_iota(jnp.int32, gram.shape, 1)
    strict = jnp.where(row > column, gram, 0.0)
    diagonal = jnp.sum(jnp.where(row == column, gram, 0.0), axis=1, keepdims=True) * 0.5
    inverse = 1.0 / diagonal
    tiles = panel // 8
    values = [jnp.concatenate([blocks_ref[j, sketch_rows + 8 * b:sketch_rows + 8 * b + 8, :] for j in range(blocks)], axis=1)
              for b in range(tiles)]
    scales = [jnp.broadcast_to(inverse[8 * b:8 * b + 8, :], (8, columns)) for b in range(tiles)]
    for i in range(panel):
        b, r = divmod(i, 8)
        solved = values[b][r:r + 1, :] * scales[b][r:r + 1, :]
        for later in range(b, tiles):
            values[later] = values[later] - strict[8 * later:8 * later + 8, i:i + 1] * solved
    coupled = jnp.concatenate([values[b] * scales[b] for b in range(tiles)], axis=0)
    coupled_ref[...] = coupled
    high, low = parts_of(coupled)
    right = jnp.concatenate([high, high, low], axis=0)
    step = slab_ref.shape[0] // CHUNKS
    per = CHUNKS // 2
    stores = []
    for k in range(CHUNKS):
        rows = pl.ds(k * step, step)
        stack_ref = (top_stack_ref, low_stack_ref)[k // per]
        moved = contract(stack_ref[(k % per) * step:(k % per + 1) * step, :], right, 1, 0)
        loads[k].wait()
        updated_ref[k * step:(k + 1) * step, :] = slab_ref[k * step:(k + 1) * step, :] - moved
        stores.append(pltpu.make_async_copy(updated_ref.at[rows, :], updated_hbm.at[rows, :], out_sems.at[k]))
        stores[-1].start()
    correction = contract(panel_sketch, coupled, 0, 0, HIGHEST)
    for j in range(blocks):
        lanes = slice(j * LANES, (j + 1) * LANES)
        sketch_next_ref[:, lanes] = (blocks_ref[j, :sketch_rows, :] - correction[:, lanes]) * scale
    for copy in stores:
        copy.wait()


def local(slab, reflectors, sketch):
    depth, columns = slab.shape
    sketch_rows = sketch.shape[0]
    cols, lines = lax.axis_size("col"), lax.axis_size("z")
    own = reflectors.shape[1]
    panel = own * cols
    total_rows = depth * lines * CORES
    blocks = columns // LANES
    core = lax.axis_index("core").astype(jnp.int32).reshape(1)
    vmem, smem, free = (pl.BlockSpec(memory_space=space) for space in (pltpu.VMEM, pltpu.SMEM, pl.ANY))
    f32, bf16 = jnp.float32, jnp.bfloat16

    def call(kernel, name, out, in_specs, out_specs=vmem, scratch=(), flops=0, moved=0, grant=SMALL_VMEM, dtypes=None):
        if isinstance(out, tuple):
            shapes = jax.ShapeDtypeStruct(out, dtypes or f32)
        else:
            shapes = [jax.ShapeDtypeStruct(shape, dtype) for shape, dtype in zip(out, dtypes or [f32] * len(out))]
        return pl.pallas_call(
            kernel, out_shape=shapes, in_specs=in_specs, out_specs=out_specs, scratch_shapes=list(scratch),
            compiler_params=pltpu.CompilerParams(vmem_limit_bytes=grant),
            cost_estimate=pl.CostEstimate(flops=flops, bytes_accessed=moved, transcendentals=0), name=name)

    dma = pltpu.SemaphoreType.DMA((CHUNKS,))
    whole = pltpu.VMEM((depth, columns), f32)
    slab_bytes = depth * columns * 4

    spread = call(spread_kernel, "spread", (cols, own, depth), [vmem])(reflectors.T)
    gathered = lax.all_to_all(spread, "col", 0, 0, tiled=True)
    sketch_slab, high, low = call(
        sketch_slab_kernel, "sketch_slab", [(sketch_rows, columns), slab.shape, slab.shape], [vmem, free], [vmem] * 3, [whole, dma],
        flops=12 * sketch_rows * depth * columns, moved=2 * slab_bytes, grant=LARGE_VMEM, dtypes=[f32, bf16, bf16])(sketch, slab)

    rows = sketch_rows + panel + panel // blocks
    pairs = blocks // CORES * rows // PAIR
    mine, other = call(
        products_kernel, "products", [(pairs, PAIR, LANES)] * 2, [smem] + [vmem] * 5, [vmem, vmem],
        [pltpu.VMEM((panel, depth), f32), pltpu.VMEM((blocks, rows, LANES), f32)],
        flops=6 * panel * depth * columns, moved=slab_bytes, grant=LARGE_VMEM)(core, gathered, sketch, sketch_slab, high, low)

    def stack(first, after):
        count = depth // 2
        return call(
            lambda *refs: stack_kernel(first, *refs), "panel_parts", (count, 3 * panel), [free, vmem],
            scratch=[pltpu.VMEM((panel, count), f32)], flops=100 * panel * count, moved=panel * count * 10, dtypes=bf16)(after, gathered)

    got = lax.ppermute(other, "core", SWAP)
    sums = call(add_kernel, "add_cores", mine.shape, [vmem, vmem])(mine, got).reshape(lines, pairs // lines, PAIR, LANES)
    parts = lax.all_to_all(sums, "z", 0, 0, tiled=True)
    top_stack = stack(0, sums)
    summed = call(sum_kernel, "sum_parts", parts.shape, [vmem, free])(parts, top_stack)
    whole_sums = lax.all_to_all(summed, "z", 0, 0, tiled=True)
    low_stack = stack(depth // 2, summed)
    mine = call(pass_kernel, "pass_on", mine.shape, [vmem, free])(whole_sums.reshape(mine.shape), low_stack)
    other = lax.ppermute(mine, "core", SWAP)

    scale = (sketch_rows / total_rows) ** 0.5
    updated, coupled, sketch_next = call(
        lambda *refs: update_kernel(scale, *refs), "solve_update", [slab.shape, (panel, columns), (sketch_rows, columns)],
        [smem] + [vmem] * 4 + [free], [free, vmem, vmem],
        [whole, whole, pltpu.VMEM((blocks, rows, LANES), f32), dma, dma],
        flops=6 * panel * depth * columns, moved=2 * slab_bytes, grant=LARGE_VMEM)(core, mine, other, top_stack, low_stack, slab)
    return (updated, coupled, sketch_next)


def solution(mesh):
    split = Mesh(mesh.devices.reshape(-1, CORES, mesh.devices.shape[1]), ("z", "core", "col"))
    row = ("z", "core")
    in_specs = (P(row, "col"), P(row, "col"), P(None, row))
    out_specs = (P(row, "col"), P(None, "col"), P(None, "col"))
    return jax.shard_map(local, mesh=split, in_specs=in_specs, out_specs=out_specs, check_vma=False)
```

```python
import jax
import jax.numpy as jnp
from jax import lax
from jax.experimental import pallas as pl
from jax.experimental.pallas import tpu as pltpu
from jax.sharding import Mesh, PartitionSpec as P

CORES = 2
CHUNKS = 4
LANES = 128
PAIR = 2
ALL_VMEM = 60 * 1024 * 1024
LARGE_VMEM = 52 * 1024 * 1024
MIDDLE_VMEM = 16 * 1024 * 1024
SMALL_VMEM = 8 * 1024 * 1024
HIGHEST = lax.Precision.HIGHEST
SWAP = [(0, 1), (1, 0)]


def contract(left, right, left_dim, right_dim, precision=None):
    return lax.dot_general(left, right, (((left_dim,), (right_dim,)), ((), ())), precision=precision, preferred_element_type=jnp.float32)


def parts_of(value):
    high = value.astype(jnp.bfloat16)
    return high, (value - high.astype(jnp.float32)).astype(jnp.bfloat16)


def start_loads(source, target, sems):
    step = source.shape[0] // CHUNKS
    copies = []
    for k in range(CHUNKS):
        rows = pl.ds(k * step, step)
        copies.append(pltpu.make_async_copy(source.at[rows, :], target.at[rows, :], sems.at[k]))
        copies[-1].start()
    return copies


def lay_panel(gathered_ref, panel_ref):
    own = gathered_ref.shape[1]
    for k in range(gathered_ref.shape[0]):
        panel_ref[k * own:(k + 1) * own, :] = gathered_ref[k, :, :panel_ref.shape[1]]


def spread_kernel(own_ref, out_ref):
    for k in range(out_ref.shape[0]):
        out_ref[k] = own_ref[...]


def sketch_slab_kernel(core_ref, sketch_ref, slab_ref, mine_ref, other_ref, high_ref, low_ref, halves_ref):
    step = slab_ref.shape[0] // CHUNKS
    sketch_rows = sketch_ref.shape[0]
    sketch_high, sketch_low = parts_of(sketch_ref[...])
    both = jnp.concatenate([sketch_high, sketch_low], axis=0)
    total = None
    for k in range(CHUNKS):
        rows = slice(k * step, (k + 1) * step)
        high, low = parts_of(slab_ref[rows, :])
        high_ref[rows, :] = high
        low_ref[rows, :] = low
        wide = contract(both[:, rows], high, 1, 0)
        term = wide[:sketch_rows] + (wide[sketch_rows:] + contract(sketch_high[:, rows], low, 1, 0))
        total = term if total is None else total + term
    half = sketch_rows // CORES
    for c in range(CORES):
        halves_ref[c] = total[c * half:(c + 1) * half, :]
    core = core_ref[0]
    for out, owner in ((other_ref, 1 - core), (mine_ref, core)):
        for p in range(out.shape[0]):
            for j in range(out.shape[1]):
                out[p, j] = halves_ref[owner, PAIR * p:PAIR * (p + 1), j * LANES:(j + 1) * LANES]


def products_kernel(is_mine, core_ref, gathered_ref, sketch_ref, high_ref, low_ref, after_ref, out_ref, panel_ref):
    del after_ref
    lay_panel(gathered_ref, panel_ref)
    panel = panel_ref.shape[0]
    count = high_ref.shape[1] // CORES
    blocks = count // LANES
    owner = core_ref[0] if is_mine else 1 - core_ref[0]
    columns = pl.ds(pl.multiple_of(owner * count, count), count)
    share = panel // CORES
    some_high, some_low = parts_of(panel_ref[pl.ds(pl.multiple_of(owner * share, share), share), :])
    some = jnp.concatenate([some_high, some_low], axis=0)
    sketch_high, sketch_low = parts_of(sketch_ref[...])
    wide = contract(some, sketch_high, 1, 1)
    panel_sketch = wide[:share] + (wide[share:] + contract(some_high, sketch_low, 1, 1))
    panel_high, panel_low = parts_of(panel_ref[...])
    both = jnp.concatenate([panel_high, panel_low], axis=0)
    wide = contract(both, high_ref[:, columns], 1, 0)
    projection = wide[:panel] + (wide[panel:] + contract(panel_high, low_ref[:, columns], 1, 0))
    folded = share // blocks
    pairs = (panel + folded) // PAIR
    for t in range(blocks):
        for i in range(panel // PAIR):
            out_ref[t * pairs + i] = projection[PAIR * i:PAIR * (i + 1), t * LANES:(t + 1) * LANES]
        for i in range(folded // PAIR):
            first = t * folded + PAIR * i
            out_ref[t * pairs + panel // PAIR + i] = panel_sketch[first:first + PAIR, :]


def join_kernel(mine_sketch_ref, got_sketch_ref, mine_ref, got_ref, out_ref):
    pieces = out_ref.shape[0]
    tall, blocks = mine_sketch_ref.shape[:2]
    tall = tall // pieces
    per = mine_ref.shape[0] // pieces
    for k in range(pieces):
        for p in range(tall):
            out_ref[k, p * blocks:(p + 1) * blocks] = mine_sketch_ref[k * tall + p] + got_sketch_ref[k * tall + p]
        span = slice(k * per, (k + 1) * per)
        out_ref[k, tall * blocks:] = mine_ref[span] + got_ref[span]


def stack_kernel(first, after_ref, gathered_ref, out_ref, panel_ref):
    del after_ref
    own = gathered_ref.shape[1]
    count = out_ref.shape[0]
    for k in range(gathered_ref.shape[0]):
        panel_ref[k * own:(k + 1) * own, :] = gathered_ref[k, :, first:first + count]
    value = panel_ref[...]
    high = value.astype(jnp.bfloat16).astype(jnp.float32)
    out_ref[...] = jnp.concatenate([high, value - high, high], axis=0).T.astype(jnp.bfloat16)


def sum_kernel(parts_ref, after_ref, out_ref):
    del after_ref
    total = parts_ref[0]
    for k in range(1, parts_ref.shape[0]):
        total = total + parts_ref[k]
    for k in range(out_ref.shape[0]):
        out_ref[k] = total


def pass_kernel(value_ref, after_ref, out_ref):
    del after_ref
    out_ref[...] = value_ref[...]


def update_kernel(scale, core_ref, mine_ref, other_ref, top_stack_ref, low_stack_ref, slab_hbm, updated_hbm, coupled_ref, sketch_next_ref,
                  slab_ref, updated_ref, blocks_ref, halves_ref, in_sems, out_sems):
    loads = start_loads(slab_hbm, slab_ref, in_sems)
    core = core_ref[0]
    sketch_rows, columns = sketch_next_ref.shape
    panel = coupled_ref.shape[0]
    blocks = blocks_ref.shape[0]
    half = blocks // CORES
    pairs = blocks_ref.shape[1] // PAIR
    pieces = mine_ref.shape[0]
    per = half * pairs // pieces
    tall = (mine_ref.shape[1] - per) // blocks
    for ref, owner in ((mine_ref, core), (other_ref, 1 - core)):
        for t in range(half):
            for i in range(pairs):
                k, place = divmod(t * pairs + i, per)
                blocks_ref[owner * half + t, PAIR * i:PAIR * (i + 1), :] = ref[k, tall * blocks + place]
    panel_sketch = jnp.concatenate([blocks_ref[j, panel:, :] for j in range(blocks)], axis=0)
    gram = contract(panel_sketch, panel_sketch, 1, 1, HIGHEST)
    row = lax.broadcasted_iota(jnp.int32, gram.shape, 0)
    column = lax.broadcasted_iota(jnp.int32, gram.shape, 1)
    strict = jnp.where(row > column, gram, 0.0)
    diagonal = jnp.sum(jnp.where(row == column, gram, 0.0), axis=1, keepdims=True) * 0.5
    inverse = 1.0 / diagonal
    tiles = panel // 8
    values = [jnp.concatenate([blocks_ref[j, 8 * b:8 * b + 8, :] for j in range(blocks)], axis=1) for b in range(tiles)]
    scales = [jnp.broadcast_to(inverse[8 * b:8 * b + 8, :], (8, columns)) for b in range(tiles)]
    for i in range(panel):
        b, r = divmod(i, 8)
        solved = values[b][r:r + 1, :] * scales[b][r:r + 1, :]
        for later in range(b, tiles):
            values[later] = values[later] - strict[8 * later:8 * later + 8, i:i + 1] * solved
    coupled = jnp.concatenate([values[b] * scales[b] for b in range(tiles)], axis=0)
    coupled_ref[...] = coupled
    high, low = parts_of(coupled)
    right = jnp.concatenate([high, high, low], axis=0)
    step = slab_ref.shape[0] // CHUNKS
    part = CHUNKS // 2
    stores = []
    for k in range(CHUNKS):
        rows = pl.ds(k * step, step)
        stack_ref = (top_stack_ref, low_stack_ref)[k // part]
        moved = contract(stack_ref[(k % part) * step:(k % part + 1) * step, :], right, 1, 0)
        loads[k].wait()
        updated_ref[k * step:(k + 1) * step, :] = slab_ref[k * step:(k + 1) * step, :] - moved
        stores.append(pltpu.make_async_copy(updated_ref.at[rows, :], updated_hbm.at[rows, :], out_sems.at[k]))
        stores[-1].start()
    count = sketch_rows // CORES
    for ref, owner in ((mine_ref, core), (other_ref, 1 - core)):
        for k in range(pieces):
            for p in range(tall):
                first = (k * tall + p) * PAIR
                for j in range(blocks):
                    halves_ref[owner, first:first + PAIR, j * LANES:(j + 1) * LANES] = ref[k, p * blocks + j]
    correction = contract(panel_sketch, coupled, 0, 0, HIGHEST)
    for c in range(CORES):
        span = slice(c * count, (c + 1) * count)
        sketch_next_ref[span, :] = (halves_ref[c] - correction[span, :]) * scale
    for copy in stores:
        copy.wait()


def local(slab, reflectors, sketch):
    depth, columns = slab.shape
    sketch_rows = sketch.shape[0]
    cols, lines = lax.axis_size("col"), lax.axis_size("z")
    own = reflectors.shape[1]
    panel = own * cols
    total_rows = depth * lines * CORES
    blocks = columns // LANES
    core = lax.axis_index("core").astype(jnp.int32).reshape(1)
    vmem, smem, free = (pl.BlockSpec(memory_space=space) for space in (pltpu.VMEM, pltpu.SMEM, pl.ANY))
    f32, bf16 = jnp.float32, jnp.bfloat16

    def call(kernel, name, out, in_specs, out_specs=vmem, scratch=(), flops=0, moved=0, grant=SMALL_VMEM, dtypes=None):
        if isinstance(out, tuple):
            shapes = jax.ShapeDtypeStruct(out, dtypes or f32)
        else:
            shapes = [jax.ShapeDtypeStruct(shape, dtype) for shape, dtype in zip(out, dtypes or [f32] * len(out))]
        return pl.pallas_call(
            kernel, out_shape=shapes, in_specs=in_specs, out_specs=out_specs, scratch_shapes=list(scratch),
            compiler_params=pltpu.CompilerParams(vmem_limit_bytes=grant),
            cost_estimate=pl.CostEstimate(flops=flops, bytes_accessed=moved, transcendentals=0), name=name)

    dma = pltpu.SemaphoreType.DMA((CHUNKS,))
    whole = pltpu.VMEM((depth, columns), f32)
    slab_bytes = depth * columns * 4

    spread = call(spread_kernel, "spread", (cols, own, depth), [vmem], grant=ALL_VMEM)(reflectors.T)
    gathered = lax.all_to_all(spread, "col", 0, 0, tiled=True)

    half_rows = sketch_rows // CORES
    sketch_half = (half_rows // PAIR, blocks, PAIR, LANES)
    mine_sketch, other_sketch, high, low = call(
        sketch_slab_kernel, "sketch_slab", [sketch_half, sketch_half, slab.shape, slab.shape], [smem, vmem, vmem], [vmem] * 4,
        [pltpu.VMEM((CORES, half_rows, columns), f32)],
        flops=6 * sketch_rows * depth * columns, moved=2 * slab_bytes, grant=MIDDLE_VMEM, dtypes=[f32, f32, bf16, bf16])(core, sketch, slab)
    got_sketch = lax.ppermute(other_sketch, "core", SWAP)

    rows = panel + panel // blocks
    pairs = blocks // CORES * rows // PAIR

    def products(is_mine, after):
        return call(
            lambda *refs: products_kernel(is_mine, *refs), "products", (pairs, PAIR, LANES), [smem] + [vmem] * 4 + [free], vmem,
            [pltpu.VMEM((panel, depth), f32)],
            flops=3 * panel * depth * columns, moved=slab_bytes, grant=MIDDLE_VMEM)(core, gathered, sketch, high, low, after)

    def stack(first, after):
        count = depth // 2
        return call(
            lambda *refs: stack_kernel(first, *refs), "panel_parts", (count, 3 * panel), [free, vmem],
            scratch=[pltpu.VMEM((panel, count), f32)], flops=100 * panel * count, moved=panel * count * 10, dtypes=bf16)(after, gathered)

    other = products(False, core)
    got = lax.ppermute(other, "core", SWAP)
    mine = products(True, other)
    per = pairs // lines
    width = half_rows // PAIR // lines * blocks + per
    sums = call(join_kernel, "join", (lines, width, PAIR, LANES), [vmem] * 4)(mine_sketch, got_sketch, mine, got)
    parts = lax.all_to_all(sums, "z", 0, 0, tiled=True)
    top_stack = stack(0, sums)
    summed = call(sum_kernel, "sum_parts", parts.shape, [vmem, free])(parts, top_stack)
    whole_sums = lax.all_to_all(summed, "z", 0, 0, tiled=True)
    low_stack = stack(depth // 2, summed)
    mine = call(pass_kernel, "pass_on", summed.shape, [vmem, free])(whole_sums, low_stack)
    other = lax.ppermute(mine, "core", SWAP)

    scale = (sketch_rows / total_rows) ** 0.5
    updated, coupled, sketch_next = call(
        lambda *refs: update_kernel(scale, *refs), "solve_update", [slab.shape, (panel, columns), (sketch_rows, columns)],
        [smem] + [vmem] * 4 + [free], [free, vmem, vmem],
        [whole, whole, pltpu.VMEM((blocks, rows, LANES), f32), pltpu.VMEM((CORES, half_rows, columns), f32), dma, dma],
        flops=6 * panel * depth * columns, moved=2 * slab_bytes, grant=LARGE_VMEM)(core, mine, other, top_stack, low_stack, slab)
    return (updated, coupled, sketch_next)


def solution(mesh):
    split = Mesh(mesh.devices.reshape(-1, CORES, mesh.devices.shape[1]), ("z", "core", "col"))
    row = ("z", "core")
    in_specs = (P(row, "col"), P(row, "col"), P(None, row))
    out_specs = (P(row, "col"), P(None, "col"), P(None, "col"))
    return jax.shard_map(local, mesh=split, in_specs=in_specs, out_specs=out_specs, check_vma=False)
```

```python
import jax
import jax.numpy as jnp
from jax import lax
from jax.experimental import pallas as pl
from jax.experimental.pallas import tpu as pltpu
from jax.sharding import Mesh, PartitionSpec as P

CORES = 2
NEAR = 2
CHUNKS = 4
LANES = 128
PAIR = 2
ALL_VMEM = 60 * 1024 * 1024
LARGE_VMEM = 52 * 1024 * 1024
MIDDLE_VMEM = 16 * 1024 * 1024
SMALL_VMEM = 8 * 1024 * 1024
HIGHEST = lax.Precision.HIGHEST
SWAP = [(0, 1), (1, 0)]


def contract(left, right, left_dim, right_dim, precision=None):
    return lax.dot_general(left, right, (((left_dim,), (right_dim,)), ((), ())), precision=precision, preferred_element_type=jnp.float32)


def parts_of(value):
    high = value.astype(jnp.bfloat16)
    return high, (value - high.astype(jnp.float32)).astype(jnp.bfloat16)


def start_loads(source, target, sems):
    step = source.shape[0] // CHUNKS
    copies = []
    for k in range(CHUNKS):
        rows = pl.ds(k * step, step)
        copies.append(pltpu.make_async_copy(source.at[rows, :], target.at[rows, :], sems.at[k]))
        copies[-1].start()
    return copies


def lay_panel(gathered_ref, panel_ref):
    own = gathered_ref.shape[1]
    for k in range(gathered_ref.shape[0]):
        panel_ref[k * own:(k + 1) * own, :] = gathered_ref[k, :, :panel_ref.shape[1]]


def spread_kernel(own_ref, out_ref):
    for k in range(out_ref.shape[0]):
        out_ref[k] = own_ref[...]


def sketch_slab_kernel(core_ref, sketch_ref, slab_ref, mine_ref, other_ref, high_ref, low_ref, halves_ref):
    step = slab_ref.shape[0] // CHUNKS
    sketch_rows = sketch_ref.shape[0]
    sketch_high, sketch_low = parts_of(sketch_ref[...])
    both = jnp.concatenate([sketch_high, sketch_low], axis=0)
    total = None
    for k in range(CHUNKS):
        rows = slice(k * step, (k + 1) * step)
        high, low = parts_of(slab_ref[rows, :])
        high_ref[rows, :] = high
        low_ref[rows, :] = low
        wide = contract(both[:, rows], high, 1, 0)
        term = wide[:sketch_rows] + (wide[sketch_rows:] + contract(sketch_high[:, rows], low, 1, 0))
        total = term if total is None else total + term
    half = sketch_rows // CORES
    for c in range(CORES):
        halves_ref[c] = total[c * half:(c + 1) * half, :]
    core = core_ref[0]
    for out, owner in ((other_ref, 1 - core), (mine_ref, core)):
        for p in range(out.shape[0]):
            for j in range(out.shape[1]):
                out[p, j] = halves_ref[owner, PAIR * p:PAIR * (p + 1), j * LANES:(j + 1) * LANES]


def split_kernel(near_ref, mine_ref, got_ref, keep_ref, send_ref):
    near, count = near_ref[0], keep_ref.shape[0]
    for out, side in ((send_ref, 1 - near), (keep_ref, near)):
        span = pl.ds(side * count, count)
        out[...] = mine_ref[span] + got_ref[span]


def products_kernel(is_mine, core_ref, gathered_ref, sketch_ref, high_ref, low_ref, after_ref, out_ref, panel_ref):
    del after_ref
    lay_panel(gathered_ref, panel_ref)
    panel = panel_ref.shape[0]
    count = high_ref.shape[1] // CORES
    blocks = count // LANES
    owner = core_ref[0] if is_mine else 1 - core_ref[0]
    columns = pl.ds(pl.multiple_of(owner * count, count), count)
    share = panel // CORES
    some_high, some_low = parts_of(panel_ref[pl.ds(pl.multiple_of(owner * share, share), share), :])
    some = jnp.concatenate([some_high, some_low], axis=0)
    sketch_high, sketch_low = parts_of(sketch_ref[...])
    wide = contract(some, sketch_high, 1, 1)
    panel_sketch = wide[:share] + (wide[share:] + contract(some_high, sketch_low, 1, 1))
    panel_high, panel_low = parts_of(panel_ref[...])
    both = jnp.concatenate([panel_high, panel_low], axis=0)
    wide = contract(both, high_ref[:, columns], 1, 0)
    projection = wide[:panel] + (wide[panel:] + contract(panel_high, low_ref[:, columns], 1, 0))
    folded = share // blocks
    pairs = (panel + folded) // PAIR
    for t in range(blocks):
        for i in range(panel // PAIR):
            out_ref[t * pairs + i] = projection[PAIR * i:PAIR * (i + 1), t * LANES:(t + 1) * LANES]
        for i in range(folded // PAIR):
            first = t * folded + PAIR * i
            out_ref[t * pairs + panel // PAIR + i] = panel_sketch[first:first + PAIR, :]


def join_kernel(keep_ref, got_sketch_ref, mine_ref, got_ref, after_ref, out_ref):
    del after_ref
    pieces, width = keep_ref.shape[:2]
    per = mine_ref.shape[0] // pieces
    for k in range(pieces):
        out_ref[k, :width] = keep_ref[k] + got_sketch_ref[k]
        span = slice(k * per, (k + 1) * per)
        out_ref[k, width:] = mine_ref[span] + got_ref[span]


def stack_kernel(after_ref, gathered_ref, out_ref, panel_ref):
    del after_ref
    lay_panel(gathered_ref, panel_ref)
    step = panel_ref.shape[1] // CHUNKS
    for k in range(CHUNKS):
        value = panel_ref[:, k * step:(k + 1) * step]
        high = value.astype(jnp.bfloat16).astype(jnp.float32)
        out_ref[k * step:(k + 1) * step, :] = jnp.concatenate([high, value - high, high], axis=0).T.astype(jnp.bfloat16)


def sum_kernel(width, parts_ref, out_ref):
    sides = [parts_ref[n] for n in range(NEAR)]
    for k in range(NEAR, parts_ref.shape[0]):
        sides[k % NEAR] = sides[k % NEAR] + parts_ref[k]
    total = sides[0]
    for side in sides[1:]:
        total = total + side
    for k in range(out_ref.shape[0]):
        for n in range(NEAR):
            out_ref[k, n * width:(n + 1) * width] = sides[n][:width]
        out_ref[k, NEAR * width:] = total[width:]


def update_kernel(scale, core_ref, mine_ref, other_ref, stack_ref, slab_hbm, updated_hbm, coupled_ref, sketch_next_ref,
                  slab_ref, updated_ref, blocks_ref, halves_ref, in_sems, out_sems):
    loads = start_loads(slab_hbm, slab_ref, in_sems)
    core = core_ref[0]
    sketch_rows, columns = sketch_next_ref.shape
    panel = coupled_ref.shape[0]
    blocks = blocks_ref.shape[0]
    half = blocks // CORES
    pairs = blocks_ref.shape[1] // PAIR
    pieces = mine_ref.shape[0]
    per = half * pairs // pieces
    for ref, owner in ((mine_ref, core), (other_ref, 1 - core)):
        for t in range(half):
            for i in range(pairs):
                k, place = divmod(t * pairs + i, per)
                blocks_ref[owner * half + t, PAIR * i:PAIR * (i + 1), :] = ref[k, NEAR * blocks + place]
    panel_sketch = jnp.concatenate([blocks_ref[j, panel:, :] for j in range(blocks)], axis=0)
    gram = contract(panel_sketch, panel_sketch, 1, 1, HIGHEST)
    row = lax.broadcasted_iota(jnp.int32, gram.shape, 0)
    column = lax.broadcasted_iota(jnp.int32, gram.shape, 1)
    strict = jnp.where(row > column, gram, 0.0)
    diagonal = jnp.sum(jnp.where(row == column, gram, 0.0), axis=1, keepdims=True) * 0.5
    inverse = 1.0 / diagonal
    tiles = panel // 8
    values = [jnp.concatenate([blocks_ref[j, 8 * b:8 * b + 8, :] for j in range(blocks)], axis=1) for b in range(tiles)]
    scales = [jnp.broadcast_to(inverse[8 * b:8 * b + 8, :], (8, columns)) for b in range(tiles)]
    for i in range(panel):
        b, r = divmod(i, 8)
        solved = values[b][r:r + 1, :] * scales[b][r:r + 1, :]
        for later in range(b, tiles):
            values[later] = values[later] - strict[8 * later:8 * later + 8, i:i + 1] * solved
    coupled = jnp.concatenate([values[b] * scales[b] for b in range(tiles)], axis=0)
    coupled_ref[...] = coupled
    high, low = parts_of(coupled)
    right = jnp.concatenate([high, high, low], axis=0)
    step = slab_ref.shape[0] // CHUNKS
    stores = []
    for k in range(CHUNKS):
        rows = pl.ds(k * step, step)
        moved = contract(stack_ref[k * step:(k + 1) * step, :], right, 1, 0)
        loads[k].wait()
        updated_ref[k * step:(k + 1) * step, :] = slab_ref[k * step:(k + 1) * step, :] - moved
        stores.append(pltpu.make_async_copy(updated_ref.at[rows, :], updated_hbm.at[rows, :], out_sems.at[k]))
        stores[-1].start()
    count = sketch_rows // CORES
    for ref, owner in ((mine_ref, core), (other_ref, 1 - core)):
        for k in range(pieces):
            for n in range(NEAR):
                first = n * count // NEAR + PAIR * k
                for j in range(blocks):
                    halves_ref[owner, first:first + PAIR, j * LANES:(j + 1) * LANES] = ref[k, n * blocks + j]
    correction = contract(panel_sketch, coupled, 0, 0, HIGHEST)
    for c in range(CORES):
        span = slice(c * count, (c + 1) * count)
        sketch_next_ref[span, :] = (halves_ref[c] - correction[span, :]) * scale
    for copy in stores:
        copy.wait()


def local(slab, reflectors, sketch):
    depth, columns = slab.shape
    sketch_rows = sketch.shape[0]
    cols, lines = lax.axis_size("col"), lax.axis_size("far") * NEAR
    z = ("far", "near")
    own = reflectors.shape[1]
    panel = own * cols
    total_rows = depth * lines * CORES
    blocks = columns // LANES
    core, near = (lax.axis_index(name).astype(jnp.int32).reshape(1) for name in ("core", "near"))
    vmem, smem, free = (pl.BlockSpec(memory_space=space) for space in (pltpu.VMEM, pltpu.SMEM, pl.ANY))
    f32, bf16 = jnp.float32, jnp.bfloat16

    def call(kernel, name, out, in_specs, out_specs=vmem, scratch=(), flops=0, moved=0, grant=SMALL_VMEM, dtypes=None):
        if isinstance(out, tuple):
            shapes = jax.ShapeDtypeStruct(out, dtypes or f32)
        else:
            shapes = [jax.ShapeDtypeStruct(shape, dtype) for shape, dtype in zip(out, dtypes or [f32] * len(out))]
        return pl.pallas_call(
            kernel, out_shape=shapes, in_specs=in_specs, out_specs=out_specs, scratch_shapes=list(scratch),
            compiler_params=pltpu.CompilerParams(vmem_limit_bytes=grant),
            cost_estimate=pl.CostEstimate(flops=flops, bytes_accessed=moved, transcendentals=0), name=name)

    dma = pltpu.SemaphoreType.DMA((CHUNKS,))
    whole = pltpu.VMEM((depth, columns), f32)
    slab_bytes = depth * columns * 4

    spread = call(spread_kernel, "spread", (cols, own, depth), [vmem], moved=4 * slab_bytes, grant=ALL_VMEM)(reflectors.T)
    gathered = lax.all_to_all(spread, "col", 0, 0, tiled=True)

    half_rows = sketch_rows // CORES
    sketch_half = (half_rows // PAIR, blocks, PAIR, LANES)
    sketch_quarter = (half_rows // PAIR // NEAR, blocks, PAIR, LANES)
    mine_sketch, other_sketch, high, low = call(
        sketch_slab_kernel, "sketch_slab", [sketch_half, sketch_half, slab.shape, slab.shape], [smem, vmem, vmem], [vmem] * 4,
        [pltpu.VMEM((CORES, half_rows, columns), f32)],
        flops=6 * sketch_rows * depth * columns, moved=2 * slab_bytes, grant=MIDDLE_VMEM, dtypes=[f32, f32, bf16, bf16])(core, sketch, slab)
    got = lax.ppermute(other_sketch, "core", SWAP)
    keep, send = call(split_kernel, "add_sketch", [sketch_quarter] * 2, [smem, vmem, vmem], [vmem, vmem])(near, mine_sketch, got)
    got_sketch = lax.ppermute(send, "near", SWAP)

    rows = panel + panel // blocks
    pairs = blocks // CORES * rows // PAIR

    def products(is_mine, after):
        return call(
            lambda *refs: products_kernel(is_mine, *refs), "products", (pairs, PAIR, LANES), [smem] + [vmem] * 4 + [free], vmem,
            [pltpu.VMEM((panel, depth), f32)],
            flops=3 * panel * depth * columns, moved=slab_bytes, grant=MIDDLE_VMEM)(core, gathered, sketch, high, low, after)

    other = products(False, send)
    got = lax.ppermute(other, "core", SWAP)
    mine = products(True, other)
    stack = call(
        stack_kernel, "panel_parts", (depth, 3 * panel), [free, vmem], scratch=[pltpu.VMEM((panel, depth), f32)],
        flops=100 * panel * depth, moved=panel * depth * 10, dtypes=bf16)(mine, gathered)
    per = pairs // lines
    sums = call(join_kernel, "join", (lines, blocks + per, PAIR, LANES), [vmem] * 4 + [free])(keep, got_sketch, mine, got, stack)
    parts = lax.all_to_all(sums, z, 0, 0, tiled=True)
    summed = call(
        lambda *refs: sum_kernel(blocks, *refs), "sum_parts", (lines, NEAR * blocks + per, PAIR, LANES), [vmem])(parts)
    mine = lax.all_to_all(summed, z, 0, 0, tiled=True)
    other = lax.ppermute(mine, "core", SWAP)

    scale = (sketch_rows / total_rows) ** 0.5
    updated, coupled, sketch_next = call(
        lambda *refs: update_kernel(scale, *refs), "solve_update", [slab.shape, (panel, columns), (sketch_rows, columns)],
        [smem] + [vmem] * 3 + [free], [free, vmem, vmem],
        [whole, whole, pltpu.VMEM((blocks, rows, LANES), f32), pltpu.VMEM((CORES, half_rows, columns), f32), dma, dma],
        flops=6 * panel * depth * columns, moved=2 * slab_bytes, grant=LARGE_VMEM)(core, mine, other, stack, slab)
    return (updated, coupled, sketch_next)


def solution(mesh):
    split = Mesh(mesh.devices.reshape(-1, NEAR, CORES, mesh.devices.shape[1]), ("far", "near", "core", "col"))
    row = ("far", "near", "core")
    in_specs = (P(row, "col"), P(row, "col"), P(None, row))
    out_specs = (P(row, "col"), P(None, "col"), P(None, "col"))
    return jax.shard_map(local, mesh=split, in_specs=in_specs, out_specs=out_specs, check_vma=False)
```

```python
import jax
import jax.numpy as jnp
from jax import lax
from jax.experimental import pallas as pl
from jax.experimental.pallas import tpu as pltpu
from jax.sharding import Mesh, PartitionSpec as P

CORES = 2
CHUNKS = 4
LANES = 128
PAIR = 2
ALL_VMEM = 60 * 1024 * 1024
LARGE_VMEM = 52 * 1024 * 1024
MIDDLE_VMEM = 16 * 1024 * 1024
SMALL_VMEM = 8 * 1024 * 1024
HIGHEST = lax.Precision.HIGHEST
SWAP = [(0, 1), (1, 0)]


def contract(left, right, left_dim, right_dim, precision=None):
    return lax.dot_general(left, right, (((left_dim,), (right_dim,)), ((), ())), precision=precision, preferred_element_type=jnp.float32)


def parts_of(value):
    high = value.astype(jnp.bfloat16)
    return high, (value - high.astype(jnp.float32)).astype(jnp.bfloat16)


def start_loads(source, target, sems):
    step = source.shape[0] // CHUNKS
    copies = []
    for k in range(CHUNKS):
        rows = pl.ds(k * step, step)
        copies.append(pltpu.make_async_copy(source.at[rows, :], target.at[rows, :], sems.at[k]))
        copies[-1].start()
    return copies


def lay_panel(gathered_ref, panel_ref):
    own = gathered_ref.shape[1]
    for k in range(gathered_ref.shape[0]):
        panel_ref[k * own:(k + 1) * own, :] = gathered_ref[k, :, :panel_ref.shape[1]]


def spread_kernel(own_ref, out_ref):
    for k in range(out_ref.shape[0]):
        out_ref[k] = own_ref[...]


def sketch_slab_kernel(core_ref, sketch_ref, slab_ref, mine_ref, other_ref, high_ref, low_ref, halves_ref):
    step = slab_ref.shape[0] // CHUNKS
    sketch_rows = sketch_ref.shape[0]
    sketch_high, sketch_low = parts_of(sketch_ref[...])
    both = jnp.concatenate([sketch_high, sketch_low], axis=0)
    total = None
    for k in range(CHUNKS):
        rows = slice(k * step, (k + 1) * step)
        high, low = parts_of(slab_ref[rows, :])
        high_ref[rows, :] = high
        low_ref[rows, :] = low
        wide = contract(both[:, rows], high, 1, 0)
        term = wide[:sketch_rows] + (wide[sketch_rows:] + contract(sketch_high[:, rows], low, 1, 0))
        total = term if total is None else total + term
    half = sketch_rows // CORES
    for c in range(CORES):
        halves_ref[c] = total[c * half:(c + 1) * half, :]
    core = core_ref[0]
    for out, owner in ((other_ref, 1 - core), (mine_ref, core)):
        for p in range(out.shape[0]):
            for j in range(out.shape[1]):
                out[p, j] = halves_ref[owner, PAIR * p:PAIR * (p + 1), j * LANES:(j + 1) * LANES]


def products_kernel(is_mine, core_ref, gathered_ref, sketch_ref, high_ref, low_ref, after_ref, out_ref, panel_ref):
    del after_ref
    lay_panel(gathered_ref, panel_ref)
    panel = panel_ref.shape[0]
    count = high_ref.shape[1] // CORES
    blocks = count // LANES
    owner = core_ref[0] if is_mine else 1 - core_ref[0]
    columns = pl.ds(pl.multiple_of(owner * count, count), count)
    share = panel // CORES
    some_high, some_low = parts_of(panel_ref[pl.ds(pl.multiple_of(owner * share, share), share), :])
    some = jnp.concatenate([some_high, some_low], axis=0)
    sketch_high, sketch_low = parts_of(sketch_ref[...])
    wide = contract(some, sketch_high, 1, 1)
    panel_sketch = wide[:share] + (wide[share:] + contract(some_high, sketch_low, 1, 1))
    panel_high, panel_low = parts_of(panel_ref[...])
    both = jnp.concatenate([panel_high, panel_low], axis=0)
    wide = contract(both, high_ref[:, columns], 1, 0)
    projection = wide[:panel] + (wide[panel:] + contract(panel_high, low_ref[:, columns], 1, 0))
    folded = share // blocks
    pairs = (panel + folded) // PAIR
    for t in range(blocks):
        for i in range(panel // PAIR):
            out_ref[t * pairs + i] = projection[PAIR * i:PAIR * (i + 1), t * LANES:(t + 1) * LANES]
        for i in range(folded // PAIR):
            first = t * folded + PAIR * i
            out_ref[t * pairs + panel // PAIR + i] = panel_sketch[first:first + PAIR, :]


def join_kernel(mine_sketch_ref, got_sketch_ref, mine_ref, got_ref, after_ref, out_ref):
    del after_ref
    pieces = out_ref.shape[0]
    tall, blocks = mine_sketch_ref.shape[:2]
    tall = tall // pieces
    per = mine_ref.shape[0] // pieces
    for k in range(pieces):
        for p in range(tall):
            out_ref[k, p * blocks:(p + 1) * blocks] = mine_sketch_ref[k * tall + p] + got_sketch_ref[k * tall + p]
        span = slice(k * per, (k + 1) * per)
        out_ref[k, tall * blocks:] = mine_ref[span] + got_ref[span]


def stack_kernel(after_ref, gathered_ref, out_ref, panel_ref):
    del after_ref
    lay_panel(gathered_ref, panel_ref)
    step = panel_ref.shape[1] // CHUNKS
    for k in range(CHUNKS):
        value = panel_ref[:, k * step:(k + 1) * step]
        high = value.astype(jnp.bfloat16).astype(jnp.float32)
        out_ref[k * step:(k + 1) * step, :] = jnp.concatenate([high, value - high, high], axis=0).T.astype(jnp.bfloat16)


def sum_kernel(parts_ref, out_ref):
    total = parts_ref[0]
    for k in range(1, parts_ref.shape[0]):
        total = total + parts_ref[k]
    for k in range(out_ref.shape[0]):
        out_ref[k] = total


def update_kernel(scale, core_ref, mine_ref, other_ref, stack_ref, slab_hbm, updated_hbm, coupled_ref, sketch_next_ref,
                  slab_ref, updated_ref, blocks_ref, halves_ref, in_sems, out_sems):
    loads = start_loads(slab_hbm, slab_ref, in_sems)
    core = core_ref[0]
    sketch_rows, columns = sketch_next_ref.shape
    panel = coupled_ref.shape[0]
    blocks = blocks_ref.shape[0]
    half = blocks // CORES
    pairs = blocks_ref.shape[1] // PAIR
    pieces = mine_ref.shape[0]
    per = half * pairs // pieces
    tall = (mine_ref.shape[1] - per) // blocks
    for ref, owner in ((mine_ref, core), (other_ref, 1 - core)):
        for t in range(half):
            for i in range(pairs):
                k, place = divmod(t * pairs + i, per)
                blocks_ref[owner * half + t, PAIR * i:PAIR * (i + 1), :] = ref[k, tall * blocks + place]
    panel_sketch = jnp.concatenate([blocks_ref[j, panel:, :] for j in range(blocks)], axis=0)
    gram = contract(panel_sketch, panel_sketch, 1, 1, HIGHEST)
    row = lax.broadcasted_iota(jnp.int32, gram.shape, 0)
    column = lax.broadcasted_iota(jnp.int32, gram.shape, 1)
    diagonal = jnp.where(row == column, gram, 0.0)
    inverse = 1.0 / (jnp.sum(diagonal, axis=1, keepdims=True) * 0.5)
    scaled = jnp.where(row > column, gram, 0.0) * (1.0 / (jnp.sum(diagonal, axis=0, keepdims=True) * 0.5))
    tiles = panel // 8
    values = [jnp.concatenate([blocks_ref[j, 8 * b:8 * b + 8, :] for j in range(blocks)], axis=1) for b in range(tiles)]
    scales = [jnp.broadcast_to(inverse[8 * b:8 * b + 8, :], (8, columns)) for b in range(tiles)]
    for i in range(panel):
        b, r = divmod(i, 8)
        final = values[b][r:r + 1, :]
        for later in range(b, tiles):
            values[later] = values[later] - scaled[8 * later:8 * later + 8, i:i + 1] * final
    coupled = jnp.concatenate([values[b] * scales[b] for b in range(tiles)], axis=0)
    coupled_ref[...] = coupled
    high, low = parts_of(coupled)
    right = jnp.concatenate([high, high, low], axis=0)
    step = slab_ref.shape[0] // CHUNKS
    stores = []
    for k in range(CHUNKS):
        rows = pl.ds(k * step, step)
        moved = contract(stack_ref[k * step:(k + 1) * step, :], right, 1, 0)
        loads[k].wait()
        updated_ref[k * step:(k + 1) * step, :] = slab_ref[k * step:(k + 1) * step, :] - moved
        stores.append(pltpu.make_async_copy(updated_ref.at[rows, :], updated_hbm.at[rows, :], out_sems.at[k]))
        stores[-1].start()
    count = sketch_rows // CORES
    for ref, owner in ((mine_ref, core), (other_ref, 1 - core)):
        for k in range(pieces):
            for p in range(tall):
                first = (k * tall + p) * PAIR
                for j in range(blocks):
                    halves_ref[owner, first:first + PAIR, j * LANES:(j + 1) * LANES] = ref[k, p * blocks + j]
    correction = contract(panel_sketch, coupled, 0, 0, HIGHEST)
    for c in range(CORES):
        span = slice(c * count, (c + 1) * count)
        sketch_next_ref[span, :] = (halves_ref[c] - correction[span, :]) * scale
    for copy in stores:
        copy.wait()


def local(slab, reflectors, sketch):
    depth, columns = slab.shape
    sketch_rows = sketch.shape[0]
    cols, lines = lax.axis_size("col"), lax.axis_size("z")
    own = reflectors.shape[1]
    panel = own * cols
    total_rows = depth * lines * CORES
    blocks = columns // LANES
    core = lax.axis_index("core").astype(jnp.int32).reshape(1)
    vmem, smem, free = (pl.BlockSpec(memory_space=space) for space in (pltpu.VMEM, pltpu.SMEM, pl.ANY))
    f32, bf16 = jnp.float32, jnp.bfloat16

    def call(kernel, name, out, in_specs, out_specs=vmem, scratch=(), flops=0, moved=0, grant=SMALL_VMEM, dtypes=None):
        if isinstance(out, tuple):
            shapes = jax.ShapeDtypeStruct(out, dtypes or f32)
        else:
            shapes = [jax.ShapeDtypeStruct(shape, dtype) for shape, dtype in zip(out, dtypes or [f32] * len(out))]
        return pl.pallas_call(
            kernel, out_shape=shapes, in_specs=in_specs, out_specs=out_specs, scratch_shapes=list(scratch),
            compiler_params=pltpu.CompilerParams(vmem_limit_bytes=grant),
            cost_estimate=pl.CostEstimate(flops=flops, bytes_accessed=moved, transcendentals=0), name=name)

    dma = pltpu.SemaphoreType.DMA((CHUNKS,))
    whole = pltpu.VMEM((depth, columns), f32)
    slab_bytes = depth * columns * 4

    spread = call(spread_kernel, "spread", (cols, own, depth), [vmem], moved=4 * slab_bytes, grant=ALL_VMEM)(reflectors.T)
    gathered = lax.all_to_all(spread, "col", 0, 0, tiled=True)

    half_rows = sketch_rows // CORES
    sketch_half = (half_rows // PAIR, blocks, PAIR, LANES)
    mine_sketch, other_sketch, high, low = call(
        sketch_slab_kernel, "sketch_slab", [sketch_half, sketch_half, slab.shape, slab.shape], [smem, vmem, vmem], [vmem] * 4,
        [pltpu.VMEM((CORES, half_rows, columns), f32)],
        flops=6 * sketch_rows * depth * columns, moved=2 * slab_bytes, grant=MIDDLE_VMEM, dtypes=[f32, f32, bf16, bf16])(core, sketch, slab)
    got_sketch = lax.ppermute(other_sketch, "core", SWAP)

    rows = panel + panel // blocks
    pairs = blocks // CORES * rows // PAIR

    def products(is_mine, after):
        return call(
            lambda *refs: products_kernel(is_mine, *refs), "products", (pairs, PAIR, LANES), [smem] + [vmem] * 4 + [free], vmem,
            [pltpu.VMEM((panel, depth), f32)],
            flops=3 * panel * depth * columns, moved=slab_bytes, grant=MIDDLE_VMEM)(core, gathered, sketch, high, low, after)

    other = products(False, core)
    got = lax.ppermute(other, "core", SWAP)
    mine = products(True, other)
    stack = call(
        stack_kernel, "panel_parts", (depth, 3 * panel), [free, vmem], scratch=[pltpu.VMEM((panel, depth), f32)],
        flops=100 * panel * depth, moved=panel * depth * 10, dtypes=bf16)(mine, gathered)
    per = pairs // lines
    width = half_rows // PAIR // lines * blocks + per
    sums = call(join_kernel, "join", (lines, width, PAIR, LANES), [vmem] * 4 + [free])(mine_sketch, got_sketch, mine, got, stack)
    parts = lax.all_to_all(sums, "z", 0, 0, tiled=True)
    summed = call(sum_kernel, "sum_parts", parts.shape, [vmem])(parts)
    mine = lax.all_to_all(summed, "z", 0, 0, tiled=True)
    other = lax.ppermute(mine, "core", SWAP)

    scale = (sketch_rows / total_rows) ** 0.5
    updated, coupled, sketch_next = call(
        lambda *refs: update_kernel(scale, *refs), "solve_update", [slab.shape, (panel, columns), (sketch_rows, columns)],
        [smem] + [vmem] * 3 + [free], [free, vmem, vmem],
        [whole, whole, pltpu.VMEM((blocks, rows, LANES), f32), pltpu.VMEM((CORES, half_rows, columns), f32), dma, dma],
        flops=6 * panel * depth * columns, moved=2 * slab_bytes, grant=LARGE_VMEM)(core, mine, other, stack, slab)
    return (updated, coupled, sketch_next)


def solution(mesh):
    split = Mesh(mesh.devices.reshape(-1, CORES, mesh.devices.shape[1]), ("z", "core", "col"))
    row = ("z", "core")
    in_specs = (P(row, "col"), P(row, "col"), P(None, row))
    out_specs = (P(row, "col"), P(None, "col"), P(None, "col"))
    return jax.shard_map(local, mesh=split, in_specs=in_specs, out_specs=out_specs, check_vma=False)
```

```python
import jax
import jax.numpy as jnp
from jax import lax
from jax.experimental import pallas as pl
from jax.experimental.pallas import tpu as pltpu
from jax.sharding import Mesh, PartitionSpec as P

CORES = 2
NEAR = 2
CHUNKS = 4
LANES = 128
PAIR = 2
ALL_VMEM = 60 * 1024 * 1024
LARGE_VMEM = 52 * 1024 * 1024
MIDDLE_VMEM = 16 * 1024 * 1024
SMALL_VMEM = 8 * 1024 * 1024
HIGHEST = lax.Precision.HIGHEST
SWAP = [(0, 1), (1, 0)]


def contract(left, right, left_dim, right_dim, precision=None):
    return lax.dot_general(left, right, (((left_dim,), (right_dim,)), ((), ())), precision=precision, preferred_element_type=jnp.float32)


def parts_of(value):
    high = value.astype(jnp.bfloat16)
    return high, (value - high.astype(jnp.float32)).astype(jnp.bfloat16)


def start_loads(source, target, sems):
    step = source.shape[0] // CHUNKS
    copies = []
    for k in range(CHUNKS):
        rows = pl.ds(k * step, step)
        copies.append(pltpu.make_async_copy(source.at[rows, :], target.at[rows, :], sems.at[k]))
        copies[-1].start()
    return copies


def lay_panel(gathered_ref, panel_ref):
    own = gathered_ref.shape[1]
    for k in range(gathered_ref.shape[0]):
        panel_ref[k * own:(k + 1) * own, :] = gathered_ref[k, :, :panel_ref.shape[1]]


def spread_kernel(own_ref, out_ref):
    for k in range(out_ref.shape[0]):
        out_ref[k] = own_ref[...]


def sketch_slab_kernel(near_ref, sketch_ref, slab_ref, mine_ref, other_ref, high_ref, low_ref, halves_ref):
    step = slab_ref.shape[0] // CHUNKS
    sketch_rows = sketch_ref.shape[0]
    sketch_high, sketch_low = parts_of(sketch_ref[...])
    both = jnp.concatenate([sketch_high, sketch_low], axis=0)
    total = None
    for k in range(CHUNKS):
        rows = slice(k * step, (k + 1) * step)
        high, low = parts_of(slab_ref[rows, :])
        high_ref[rows, :] = high
        low_ref[rows, :] = low
        wide = contract(both[:, rows], high, 1, 0)
        term = wide[:sketch_rows] + (wide[sketch_rows:] + contract(sketch_high[:, rows], low, 1, 0))
        total = term if total is None else total + term
    half = sketch_rows // NEAR
    for c in range(NEAR):
        halves_ref[c] = total[c * half:(c + 1) * half, :]
    near = near_ref[0]
    for out, owner in ((other_ref, 1 - near), (mine_ref, near)):
        for p in range(out.shape[0]):
            for j in range(out.shape[1]):
                out[p, j] = halves_ref[owner, PAIR * p:PAIR * (p + 1), j * LANES:(j + 1) * LANES]


def pack_kernel(core_ref, mine_sketch_ref, got_sketch_ref, other_ref, send_ref, keep_ref):
    core = core_ref[0]
    pieces, width = keep_ref.shape[:2]
    per = other_ref.shape[0] // pieces
    span = pl.ds(core * pieces, pieces)
    keep_ref[...] = mine_sketch_ref[span] + got_sketch_ref[span]
    first = (1 - core) * pieces
    for k in range(pieces):
        send_ref[k, :width] = mine_sketch_ref[first + k] + got_sketch_ref[first + k]
        send_ref[k, width:] = other_ref[k * per:(k + 1) * per]


def products_kernel(is_mine, core_ref, gathered_ref, sketch_ref, high_ref, low_ref, after_ref, out_ref, panel_ref):
    del after_ref
    lay_panel(gathered_ref, panel_ref)
    panel = panel_ref.shape[0]
    count = high_ref.shape[1] // CORES
    blocks = count // LANES
    owner = core_ref[0] if is_mine else 1 - core_ref[0]
    columns = pl.ds(pl.multiple_of(owner * count, count), count)
    share = panel // CORES
    some_high, some_low = parts_of(panel_ref[pl.ds(pl.multiple_of(owner * share, share), share), :])
    some = jnp.concatenate([some_high, some_low], axis=0)
    sketch_high, sketch_low = parts_of(sketch_ref[...])
    wide = contract(some, sketch_high, 1, 1)
    panel_sketch = wide[:share] + (wide[share:] + contract(some_high, sketch_low, 1, 1))
    panel_high, panel_low = parts_of(panel_ref[...])
    both = jnp.concatenate([panel_high, panel_low], axis=0)
    wide = contract(both, high_ref[:, columns], 1, 0)
    projection = wide[:panel] + (wide[panel:] + contract(panel_high, low_ref[:, columns], 1, 0))
    folded = share // blocks
    pairs = (panel + folded) // PAIR
    for t in range(blocks):
        for i in range(panel // PAIR):
            out_ref[t * pairs + i] = projection[PAIR * i:PAIR * (i + 1), t * LANES:(t + 1) * LANES]
        for i in range(folded // PAIR):
            first = t * folded + PAIR * i
            out_ref[t * pairs + panel // PAIR + i] = panel_sketch[first:first + PAIR, :]


def join_kernel(keep_ref, mine_ref, got_ref, after_ref, out_ref):
    del after_ref
    pieces, width = keep_ref.shape[:2]
    per = mine_ref.shape[0] // pieces
    for k in range(pieces):
        out_ref[k, :width] = keep_ref[k] + got_ref[k, :width]
        out_ref[k, width:] = mine_ref[k * per:(k + 1) * per] + got_ref[k, width:]


def stack_kernel(after_ref, gathered_ref, out_ref, panel_ref):
    del after_ref
    lay_panel(gathered_ref, panel_ref)
    step = panel_ref.shape[1] // CHUNKS
    for k in range(CHUNKS):
        value = panel_ref[:, k * step:(k + 1) * step]
        high = value.astype(jnp.bfloat16).astype(jnp.float32)
        out_ref[k * step:(k + 1) * step, :] = jnp.concatenate([high, value - high, high], axis=0).T.astype(jnp.bfloat16)


def sum_kernel(width, parts_ref, out_ref):
    sides = [parts_ref[n] for n in range(NEAR)]
    for k in range(NEAR, parts_ref.shape[0]):
        sides[k % NEAR] = sides[k % NEAR] + parts_ref[k]
    total = sides[0]
    for side in sides[1:]:
        total = total + side
    for k in range(out_ref.shape[0]):
        for n in range(NEAR):
            out_ref[k, n * width:(n + 1) * width] = sides[n][:width]
        out_ref[k, NEAR * width:] = total[width:]


def update_kernel(scale, core_ref, mine_ref, other_ref, stack_ref, slab_hbm, updated_hbm, coupled_ref, sketch_next_ref,
                  slab_ref, updated_ref, blocks_ref, halves_ref, in_sems, out_sems):
    loads = start_loads(slab_hbm, slab_ref, in_sems)
    core = core_ref[0]
    sketch_rows, columns = sketch_next_ref.shape
    panel = coupled_ref.shape[0]
    blocks = blocks_ref.shape[0]
    half = blocks // CORES
    pairs = blocks_ref.shape[1] // PAIR
    pieces = mine_ref.shape[0]
    per = half * pairs // pieces
    for ref, owner in ((mine_ref, core), (other_ref, 1 - core)):
        for t in range(half):
            for i in range(pairs):
                k, place = divmod(t * pairs + i, per)
                blocks_ref[owner * half + t, PAIR * i:PAIR * (i + 1), :] = ref[k, NEAR * blocks + place]
    panel_sketch = jnp.concatenate([blocks_ref[j, panel:, :] for j in range(blocks)], axis=0)
    gram = contract(panel_sketch, panel_sketch, 1, 1, HIGHEST)
    row = lax.broadcasted_iota(jnp.int32, gram.shape, 0)
    column = lax.broadcasted_iota(jnp.int32, gram.shape, 1)
    diagonal = jnp.where(row == column, gram, 0.0)
    inverse = 1.0 / (jnp.sum(diagonal, axis=1, keepdims=True) * 0.5)
    scaled = jnp.where(row > column, gram, 0.0) * (1.0 / (jnp.sum(diagonal, axis=0, keepdims=True) * 0.5))
    tiles = panel // 8
    values = [jnp.concatenate([blocks_ref[j, 8 * b:8 * b + 8, :] for j in range(blocks)], axis=1) for b in range(tiles)]
    scales = [jnp.broadcast_to(inverse[8 * b:8 * b + 8, :], (8, columns)) for b in range(tiles)]
    for i in range(panel):
        b, r = divmod(i, 8)
        final = values[b][r:r + 1, :]
        for later in range(b, tiles):
            values[later] = values[later] - scaled[8 * later:8 * later + 8, i:i + 1] * final
    coupled = jnp.concatenate([values[b] * scales[b] for b in range(tiles)], axis=0)
    coupled_ref[...] = coupled
    high, low = parts_of(coupled)
    right = jnp.concatenate([high, high, low], axis=0)
    step = slab_ref.shape[0] // CHUNKS
    stores = []
    for k in range(CHUNKS):
        rows = pl.ds(k * step, step)
        moved = contract(stack_ref[k * step:(k + 1) * step, :], right, 1, 0)
        loads[k].wait()
        updated_ref[k * step:(k + 1) * step, :] = slab_ref[k * step:(k + 1) * step, :] - moved
        stores.append(pltpu.make_async_copy(updated_ref.at[rows, :], updated_hbm.at[rows, :], out_sems.at[k]))
        stores[-1].start()
    count = sketch_rows // CORES
    for ref, owner in ((mine_ref, core), (other_ref, 1 - core)):
        for k in range(pieces):
            for n in range(NEAR):
                first = n * count // NEAR + PAIR * k
                for j in range(blocks):
                    halves_ref[owner, first:first + PAIR, j * LANES:(j + 1) * LANES] = ref[k, n * blocks + j]
    correction = contract(panel_sketch, coupled, 0, 0, HIGHEST)
    share = count // NEAR
    for c in range(CORES):
        for n in range(NEAR):
            span = slice((n * CORES + c) * share, (n * CORES + c + 1) * share)
            sketch_next_ref[span, :] = (halves_ref[c, n * share:(n + 1) * share, :] - correction[span, :]) * scale
    for copy in stores:
        copy.wait()


def local(slab, reflectors, sketch):
    depth, columns = slab.shape
    sketch_rows = sketch.shape[0]
    cols, lines = lax.axis_size("col"), lax.axis_size("far") * NEAR
    z = ("far", "near")
    own = reflectors.shape[1]
    panel = own * cols
    total_rows = depth * lines * CORES
    blocks = columns // LANES
    core, near = (lax.axis_index(name).astype(jnp.int32).reshape(1) for name in ("core", "near"))
    vmem, smem, free = (pl.BlockSpec(memory_space=space) for space in (pltpu.VMEM, pltpu.SMEM, pl.ANY))
    f32, bf16 = jnp.float32, jnp.bfloat16

    def call(kernel, name, out, in_specs, out_specs=vmem, scratch=(), flops=0, moved=0, grant=SMALL_VMEM, dtypes=None):
        if isinstance(out, tuple):
            shapes = jax.ShapeDtypeStruct(out, dtypes or f32)
        else:
            shapes = [jax.ShapeDtypeStruct(shape, dtype) for shape, dtype in zip(out, dtypes or [f32] * len(out))]
        return pl.pallas_call(
            kernel, out_shape=shapes, in_specs=in_specs, out_specs=out_specs, scratch_shapes=list(scratch),
            compiler_params=pltpu.CompilerParams(vmem_limit_bytes=grant),
            cost_estimate=pl.CostEstimate(flops=flops, bytes_accessed=moved, transcendentals=0), name=name)

    dma = pltpu.SemaphoreType.DMA((CHUNKS,))
    whole = pltpu.VMEM((depth, columns), f32)
    slab_bytes = depth * columns * 4

    spread = call(spread_kernel, "spread", (cols, own, depth), [vmem], moved=4 * slab_bytes, grant=ALL_VMEM)(reflectors.T)
    gathered = lax.all_to_all(spread, "col", 0, 0, tiled=True)

    half_rows = sketch_rows // CORES
    sketch_half = (half_rows // PAIR, blocks, PAIR, LANES)
    sketch_quarter = (half_rows // PAIR // NEAR, blocks, PAIR, LANES)
    mine_sketch, other_sketch, high, low = call(
        sketch_slab_kernel, "sketch_slab", [sketch_half, sketch_half, slab.shape, slab.shape], [smem, vmem, vmem], [vmem] * 4,
        [pltpu.VMEM((NEAR, half_rows, columns), f32)],
        flops=6 * sketch_rows * depth * columns, moved=2 * slab_bytes, grant=MIDDLE_VMEM, dtypes=[f32, f32, bf16, bf16])(near, sketch, slab)
    got_sketch = lax.ppermute(other_sketch, "near", SWAP)

    rows = panel + panel // blocks
    pairs = blocks // CORES * rows // PAIR

    def products(is_mine, after):
        return call(
            lambda *refs: products_kernel(is_mine, *refs), "products", (pairs, PAIR, LANES), [smem] + [vmem] * 4 + [free], vmem,
            [pltpu.VMEM((panel, depth), f32)],
            flops=3 * panel * depth * columns, moved=slab_bytes, grant=MIDDLE_VMEM)(core, gathered, sketch, high, low, after)

    other = products(False, core)
    per = pairs // lines
    send, keep = call(
        pack_kernel, "pack", [(lines, blocks + per, PAIR, LANES), sketch_quarter], [smem, vmem, vmem, vmem], [vmem, vmem])(
            core, mine_sketch, got_sketch, other)
    got = lax.ppermute(send, "core", SWAP)
    mine = products(True, send)
    stack = call(
        stack_kernel, "panel_parts", (depth, 3 * panel), [free, vmem], scratch=[pltpu.VMEM((panel, depth), f32)],
        flops=100 * panel * depth, moved=panel * depth * 10, dtypes=bf16)(mine, gathered)
    sums = call(join_kernel, "join", send.shape, [vmem] * 3 + [free])(keep, mine, got, stack)
    parts = lax.all_to_all(sums, z, 0, 0, tiled=True)
    summed = call(
        lambda *refs: sum_kernel(blocks, *refs), "sum_parts", (lines, NEAR * blocks + per, PAIR, LANES), [vmem])(parts)
    mine = lax.all_to_all(summed, z, 0, 0, tiled=True)
    other = lax.ppermute(mine, "core", SWAP)

    scale = (sketch_rows / total_rows) ** 0.5
    updated, coupled, sketch_next = call(
        lambda *refs: update_kernel(scale, *refs), "solve_update", [slab.shape, (panel, columns), (sketch_rows, columns)],
        [smem] + [vmem] * 3 + [free], [free, vmem, vmem],
        [whole, whole, pltpu.VMEM((blocks, rows, LANES), f32), pltpu.VMEM((CORES, half_rows, columns), f32), dma, dma],
        flops=6 * panel * depth * columns, moved=2 * slab_bytes, grant=LARGE_VMEM)(core, mine, other, stack, slab)
    return (updated, coupled, sketch_next)


def solution(mesh):
    split = Mesh(mesh.devices.reshape(-1, NEAR, CORES, mesh.devices.shape[1]), ("far", "near", "core", "col"))
    row = ("far", "near", "core")
    in_specs = (P(row, "col"), P(row, "col"), P(None, row))
    out_specs = (P(row, "col"), P(None, "col"), P(None, "col"))
    return jax.shard_map(local, mesh=split, in_specs=in_specs, out_specs=out_specs, check_vma=False)
```

```python
import jax
import jax.numpy as jnp
from jax import lax
from jax.experimental import pallas as pl
from jax.experimental.pallas import tpu as pltpu
from jax.sharding import Mesh, PartitionSpec as P

CORES = 2
NEAR = 2
CHUNKS = 4
LANES = 128
PAIR = 2
ALL_VMEM = 60 * 1024 * 1024
LARGE_VMEM = 52 * 1024 * 1024
MIDDLE_VMEM = 16 * 1024 * 1024
SMALL_VMEM = 8 * 1024 * 1024
HIGHEST = lax.Precision.HIGHEST
SWAP = [(0, 1), (1, 0)]


def contract(left, right, left_dim, right_dim, precision=None):
    return lax.dot_general(left, right, (((left_dim,), (right_dim,)), ((), ())), precision=precision, preferred_element_type=jnp.float32)


def parts_of(value):
    high = value.astype(jnp.bfloat16)
    return high, (value - high.astype(jnp.float32)).astype(jnp.bfloat16)


def start_loads(source, target, sems):
    step = source.shape[0] // CHUNKS
    copies = []
    for k in range(CHUNKS):
        rows = pl.ds(k * step, step)
        copies.append(pltpu.make_async_copy(source.at[rows, :], target.at[rows, :], sems.at[k]))
        copies[-1].start()
    return copies


def lay_panel(gathered_ref, panel_ref):
    own = gathered_ref.shape[1]
    for k in range(gathered_ref.shape[0]):
        panel_ref[k * own:(k + 1) * own, :] = gathered_ref[k, :, :panel_ref.shape[1]]


def spread_kernel(own_ref, out_hbm, sems):
    copies = [pltpu.make_async_copy(own_ref, out_hbm.at[k], sems.at[k]) for k in range(out_hbm.shape[0])]
    for copy in copies:
        copy.start()
    for copy in copies:
        copy.wait()


def sketch_slab_kernel(near_ref, sketch_ref, slab_ref, mine_ref, other_ref, high_ref, low_ref, halves_ref):
    step = slab_ref.shape[0] // CHUNKS
    sketch_rows = sketch_ref.shape[0]
    sketch_high, sketch_low = parts_of(sketch_ref[...])
    both = jnp.concatenate([sketch_high, sketch_low], axis=0)
    total = None
    for k in range(CHUNKS):
        rows = slice(k * step, (k + 1) * step)
        high, low = parts_of(slab_ref[rows, :])
        high_ref[rows, :] = high
        low_ref[rows, :] = low
        wide = contract(both[:, rows], high, 1, 0)
        term = wide[:sketch_rows] + (wide[sketch_rows:] + contract(sketch_high[:, rows], low, 1, 0))
        total = term if total is None else total + term
    half = sketch_rows // NEAR
    for c in range(NEAR):
        halves_ref[c] = total[c * half:(c + 1) * half, :]
    near = near_ref[0]
    for out, owner in ((other_ref, 1 - near), (mine_ref, near)):
        for p in range(out.shape[0]):
            for j in range(out.shape[1]):
                out[p, j] = halves_ref[owner, PAIR * p:PAIR * (p + 1), j * LANES:(j + 1) * LANES]


def pack_kernel(core_ref, mine_sketch_ref, got_sketch_ref, other_ref, send_ref, keep_ref):
    core = core_ref[0]
    pieces, width = keep_ref.shape[:2]
    per = other_ref.shape[0] // pieces
    span = pl.ds(core * pieces, pieces)
    keep_ref[...] = mine_sketch_ref[span] + got_sketch_ref[span]
    first = (1 - core) * pieces
    for k in range(pieces):
        send_ref[k, :width] = mine_sketch_ref[first + k] + got_sketch_ref[first + k]
        send_ref[k, width:] = other_ref[k * per:(k + 1) * per]


def products_kernel(is_mine, core_ref, gathered_ref, sketch_ref, high_ref, low_ref, after_ref, out_ref, panel_ref):
    del after_ref
    lay_panel(gathered_ref, panel_ref)
    panel = panel_ref.shape[0]
    count = high_ref.shape[1] // CORES
    blocks = count // LANES
    owner = core_ref[0] if is_mine else 1 - core_ref[0]
    columns = pl.ds(pl.multiple_of(owner * count, count), count)
    share = panel // CORES
    some_high, some_low = parts_of(panel_ref[pl.ds(pl.multiple_of(owner * share, share), share), :])
    some = jnp.concatenate([some_high, some_low], axis=0)
    sketch_high, sketch_low = parts_of(sketch_ref[...])
    wide = contract(some, sketch_high, 1, 1)
    panel_sketch = wide[:share] + (wide[share:] + contract(some_high, sketch_low, 1, 1))
    panel_high, panel_low = parts_of(panel_ref[...])
    both = jnp.concatenate([panel_high, panel_low], axis=0)
    wide = contract(both, high_ref[:, columns], 1, 0)
    projection = wide[:panel] + (wide[panel:] + contract(panel_high, low_ref[:, columns], 1, 0))
    folded = share // blocks
    pairs = (panel + folded) // PAIR
    for t in range(blocks):
        for i in range(panel // PAIR):
            out_ref[t * pairs + i] = projection[PAIR * i:PAIR * (i + 1), t * LANES:(t + 1) * LANES]
        for i in range(folded // PAIR):
            first = t * folded + PAIR * i
            out_ref[t * pairs + panel // PAIR + i] = panel_sketch[first:first + PAIR, :]


def join_kernel(keep_ref, mine_ref, got_ref, after_ref, out_ref):
    del after_ref
    pieces, width = keep_ref.shape[:2]
    per = mine_ref.shape[0] // pieces
    for k in range(pieces):
        out_ref[k, :width] = keep_ref[k] + got_ref[k, :width]
        out_ref[k, width:] = mine_ref[k * per:(k + 1) * per] + got_ref[k, width:]


def stack_kernel(after_ref, gathered_ref, out_ref, panel_ref):
    del after_ref
    lay_panel(gathered_ref, panel_ref)
    step = panel_ref.shape[1] // CHUNKS
    for k in range(CHUNKS):
        value = panel_ref[:, k * step:(k + 1) * step]
        high = value.astype(jnp.bfloat16).astype(jnp.float32)
        out_ref[k * step:(k + 1) * step, :] = jnp.concatenate([high, value - high, high], axis=0).T.astype(jnp.bfloat16)


def sum_kernel(width, parts_ref, out_ref):
    sides = [parts_ref[n] for n in range(NEAR)]
    for k in range(NEAR, parts_ref.shape[0]):
        sides[k % NEAR] = sides[k % NEAR] + parts_ref[k]
    total = sides[0]
    for side in sides[1:]:
        total = total + side
    for k in range(out_ref.shape[0]):
        for n in range(NEAR):
            out_ref[k, n * width:(n + 1) * width] = sides[n][:width]
        out_ref[k, NEAR * width:] = total[width:]


def update_kernel(scale, core_ref, mine_ref, other_ref, stack_ref, slab_hbm, updated_hbm, coupled_ref, sketch_next_ref,
                  slab_ref, updated_ref, blocks_ref, halves_ref, in_sems, out_sems):
    loads = start_loads(slab_hbm, slab_ref, in_sems)
    core = core_ref[0]
    sketch_rows, columns = sketch_next_ref.shape
    panel = coupled_ref.shape[0]
    blocks = blocks_ref.shape[0]
    half = blocks // CORES
    pairs = blocks_ref.shape[1] // PAIR
    pieces = mine_ref.shape[0]
    per = half * pairs // pieces
    for ref, owner in ((mine_ref, core), (other_ref, 1 - core)):
        for t in range(half):
            for i in range(pairs):
                k, place = divmod(t * pairs + i, per)
                blocks_ref[owner * half + t, PAIR * i:PAIR * (i + 1), :] = ref[k, NEAR * blocks + place]
    panel_sketch = jnp.concatenate([blocks_ref[j, panel:, :] for j in range(blocks)], axis=0)
    gram = contract(panel_sketch, panel_sketch, 1, 1, HIGHEST)
    row = lax.broadcasted_iota(jnp.int32, gram.shape, 0)
    column = lax.broadcasted_iota(jnp.int32, gram.shape, 1)
    diagonal = jnp.where(row == column, gram, 0.0)
    inverse = 1.0 / (jnp.sum(diagonal, axis=1, keepdims=True) * 0.5)
    scaled = jnp.where(row > column, gram, 0.0) * (1.0 / (jnp.sum(diagonal, axis=0, keepdims=True) * 0.5))
    tiles = panel // 8
    values = [jnp.concatenate([blocks_ref[j, 8 * b:8 * b + 8, :] for j in range(blocks)], axis=1) for b in range(tiles)]
    scales = [jnp.broadcast_to(inverse[8 * b:8 * b + 8, :], (8, columns)) for b in range(tiles)]
    for i in range(panel):
        b, r = divmod(i, 8)
        final = values[b][r:r + 1, :]
        for later in range(b, tiles):
            values[later] = values[later] - scaled[8 * later:8 * later + 8, i:i + 1] * final
    coupled = jnp.concatenate([values[b] * scales[b] for b in range(tiles)], axis=0)
    coupled_ref[...] = coupled
    high, low = parts_of(coupled)
    right = jnp.concatenate([high, high, low], axis=0)
    step = slab_ref.shape[0] // CHUNKS
    stores = []
    for k in range(CHUNKS):
        rows = pl.ds(k * step, step)
        moved = contract(stack_ref[k * step:(k + 1) * step, :], right, 1, 0)
        loads[k].wait()
        updated_ref[k * step:(k + 1) * step, :] = slab_ref[k * step:(k + 1) * step, :] - moved
        stores.append(pltpu.make_async_copy(updated_ref.at[rows, :], updated_hbm.at[rows, :], out_sems.at[k]))
        stores[-1].start()
    count = sketch_rows // CORES
    for ref, owner in ((mine_ref, core), (other_ref, 1 - core)):
        for k in range(pieces):
            for n in range(NEAR):
                first = n * count // NEAR + PAIR * k
                for j in range(blocks):
                    halves_ref[owner, first:first + PAIR, j * LANES:(j + 1) * LANES] = ref[k, n * blocks + j]
    correction = contract(panel_sketch, coupled, 0, 0, HIGHEST)
    share = count // NEAR
    for c in range(CORES):
        for n in range(NEAR):
            span = slice((n * CORES + c) * share, (n * CORES + c + 1) * share)
            sketch_next_ref[span, :] = (halves_ref[c, n * share:(n + 1) * share, :] - correction[span, :]) * scale
    for copy in stores:
        copy.wait()


def local(slab, reflectors, sketch):
    depth, columns = slab.shape
    sketch_rows = sketch.shape[0]
    cols, lines = lax.axis_size("col"), lax.axis_size("far") * NEAR
    z = ("far", "near")
    own = reflectors.shape[1]
    panel = own * cols
    total_rows = depth * lines * CORES
    blocks = columns // LANES
    core, near = (lax.axis_index(name).astype(jnp.int32).reshape(1) for name in ("core", "near"))
    vmem, smem, free = (pl.BlockSpec(memory_space=space) for space in (pltpu.VMEM, pltpu.SMEM, pl.ANY))
    f32, bf16 = jnp.float32, jnp.bfloat16

    def call(kernel, name, out, in_specs, out_specs=vmem, scratch=(), flops=0, moved=0, grant=SMALL_VMEM, dtypes=None):
        if isinstance(out, tuple):
            shapes = jax.ShapeDtypeStruct(out, dtypes or f32)
        else:
            shapes = [jax.ShapeDtypeStruct(shape, dtype) for shape, dtype in zip(out, dtypes or [f32] * len(out))]
        return pl.pallas_call(
            kernel, out_shape=shapes, in_specs=in_specs, out_specs=out_specs, scratch_shapes=list(scratch),
            compiler_params=pltpu.CompilerParams(vmem_limit_bytes=grant),
            cost_estimate=pl.CostEstimate(flops=flops, bytes_accessed=moved, transcendentals=0), name=name)

    dma = pltpu.SemaphoreType.DMA((CHUNKS,))
    whole = pltpu.VMEM((depth, columns), f32)
    slab_bytes = depth * columns * 4

    spread = call(spread_kernel, "spread", (cols, own, depth), [vmem], free, [pltpu.SemaphoreType.DMA((cols,))],
                  moved=4 * slab_bytes, grant=ALL_VMEM)(reflectors.T)
    gathered = lax.all_to_all(spread, "col", 0, 0, tiled=True)

    half_rows = sketch_rows // CORES
    sketch_half = (half_rows // PAIR, blocks, PAIR, LANES)
    sketch_quarter = (half_rows // PAIR // NEAR, blocks, PAIR, LANES)
    mine_sketch, other_sketch, high, low = call(
        sketch_slab_kernel, "sketch_slab", [sketch_half, sketch_half, slab.shape, slab.shape], [smem, vmem, vmem], [vmem] * 4,
        [pltpu.VMEM((NEAR, half_rows, columns), f32)],
        flops=6 * sketch_rows * depth * columns, moved=2 * slab_bytes, grant=MIDDLE_VMEM, dtypes=[f32, f32, bf16, bf16])(near, sketch, slab)
    got_sketch = lax.ppermute(other_sketch, "near", SWAP)

    rows = panel + panel // blocks
    pairs = blocks // CORES * rows // PAIR

    def products(is_mine, after):
        return call(
            lambda *refs: products_kernel(is_mine, *refs), "products", (pairs, PAIR, LANES), [smem] + [vmem] * 4 + [free], vmem,
            [pltpu.VMEM((panel, depth), f32)],
            flops=3 * panel * depth * columns, moved=slab_bytes, grant=MIDDLE_VMEM)(core, gathered, sketch, high, low, after)

    other = products(False, core)
    per = pairs // lines
    send, keep = call(
        pack_kernel, "pack", [(lines, blocks + per, PAIR, LANES), sketch_quarter], [smem, vmem, vmem, vmem], [vmem, vmem])(
            core, mine_sketch, got_sketch, other)
    got = lax.ppermute(send, "core", SWAP)
    mine = products(True, send)
    stack = call(
        stack_kernel, "panel_parts", (depth, 3 * panel), [free, vmem], scratch=[pltpu.VMEM((panel, depth), f32)],
        flops=100 * panel * depth, moved=panel * depth * 10, dtypes=bf16)(mine, gathered)
    sums = call(join_kernel, "join", send.shape, [vmem] * 3 + [free])(keep, mine, got, stack)
    parts = lax.all_to_all(sums, z, 0, 0, tiled=True)
    summed = call(
        lambda *refs: sum_kernel(blocks, *refs), "sum_parts", (lines, NEAR * blocks + per, PAIR, LANES), [vmem])(parts)
    mine = lax.all_to_all(summed, z, 0, 0, tiled=True)
    other = lax.ppermute(mine, "core", SWAP)

    scale = (sketch_rows / total_rows) ** 0.5
    updated, coupled, sketch_next = call(
        lambda *refs: update_kernel(scale, *refs), "solve_update", [slab.shape, (panel, columns), (sketch_rows, columns)],
        [smem] + [vmem] * 3 + [free], [free, vmem, vmem],
        [whole, whole, pltpu.VMEM((blocks, rows, LANES), f32), pltpu.VMEM((CORES, half_rows, columns), f32), dma, dma],
        flops=6 * panel * depth * columns, moved=2 * slab_bytes, grant=LARGE_VMEM)(core, mine, other, stack, slab)
    return (updated, coupled, sketch_next)


def solution(mesh):
    split = Mesh(mesh.devices.reshape(-1, NEAR, CORES, mesh.devices.shape[1]), ("far", "near", "core", "col"))
    row = ("far", "near", "core")
    in_specs = (P(row, "col"), P(row, "col"), P(None, row))
    out_specs = (P(row, "col"), P(None, "col"), P(None, "col"))
    return jax.shard_map(local, mesh=split, in_specs=in_specs, out_specs=out_specs, check_vma=False)
```
